256 devices in a mesh: server: 32 (over z, x), section: 2 (over core), dp: 4 (over y).
Axes of the slice: x: 4, y: 4, z: 8, core: 2. Of those that a mesh axis runs over, the one named last changes fastest.
Arguments:
- queries: bfloat16 [4, 4096, 2048], P('dp', 'server', 'section'), may hold values from -90 to 90
- key_rows: bfloat16 [4, 4096, 512], P('dp', 'server', 'section'), may hold values from -4 to 4
- saved_value_rows: bfloat16 [4, 4096, 512], P('dp', 'server', 'section'), may hold values from -5 to 5
- out_grad: bfloat16 [4, 4096, 2048], P('dp', 'server', 'section'), may hold values from -5 to 5
- doc_lens: int32 [4, 8], P('dp'), may hold values from 1 to 2048, 4096 in all within a row
- w_query: bfloat16 [4096, 2048], P('dp', 'section'), may hold values from -0.125 to 0.125
- key_weight: bfloat16 [4096, 512], P('dp', 'section'), may hold values from -0.25 to 0.25
- value_weight: bfloat16 [4096, 512], P('dp', 'section'), may hold values from -0.25 to 0.25
Outputs:
- input_grad: bfloat16 [4, 4096, 4096], P('dp', 'server')
The draws below stay inside these ranges and needn't reach their ends.
Inputs may be any that keep to these rules, and one draw needn't show every extreme that they name: `doc_lens`: each document holds at most 2048 positions.
All inputs are finite; a program needn't handle non-finite values.
Results may differ from the reference program's by a relative error of at most 0.006.
Values may be sent and summed in bfloat16 or wider, within the bound.
No kernel may reach another device: no remote copies, remote signals or barrier semaphores. Data moves between devices by JAX's collectives and lax.ppermute only.
A program may use at most 128 MiB of HBM per device.

```python
import math
import jax
import jax.numpy as jnp
import numpy as np
from jax import lax

MODEL_WIDTH = 4096
QUERY_HEADS = 16
KEY_HEADS = 4
HEAD_SIZE = 128
QUERY_PER_KV = 4
NDOC = 8
SEQUENCE_LENGTH = 4096
BATCH_COUNT = 4


def shared_normals(key):
    return jnp.clip(jax.random.normal(key, (BATCH_COUNT, SEQUENCE_LENGTH, KEY_HEADS * HEAD_SIZE), jnp.float32), -4.0, 4.0)


def draw_key_rows(key, part):
    return shared_normals(key).astype(jnp.bfloat16)


def draw_queries(key, part):
    key = jax.random.fold_in(key, 3)
    first_key = jax.random.fold_in(key, 0)
    own_rows = jnp.clip(jax.random.normal(first_key, (BATCH_COUNT, SEQUENCE_LENGTH, QUERY_HEADS * HEAD_SIZE), jnp.float32), -4.0, 4.0)
    return own_rows.astype(jnp.bfloat16)


def block_levels(rng, shape, shards, low, high):
    def one(dim, shards_of):
        draws = jax.random.uniform(jax.random.fold_in(jax.random.fold_in(rng, 6), dim), (shards_of,), jnp.float32, low / len(shards), high / len(shards))
        return jnp.repeat(jnp.exp(draws), shape[dim] // shards_of).reshape((-1,) + (1,) * (len(shape) - dim - 1))

    loudness = one(*shards[0])
    for cut in shards[1:]:
        loudness = loudness * one(*cut)
    return loudness


def length_profile(count, total, most, lean):
    loads = [(1 << 20) // math.isqrt(rank ** lean) + 1 for rank in range(2, count + 1)]
    surplus, given = total - most - (count - 1), [1] * (count - 1)
    while surplus > 0:
        free = [i for i in range(count - 1) if given[i] < most]
        whole, budget = sum([loads[i] for i in free]), surplus
        for i in free:
            addition = min(most - given[i], max(1, budget * loads[i] // whole), surplus)
            given[i] = given[i] + addition
            surplus = surplus - addition
    return np.array([most] + given)


def ragged_sizes(rng, number_of, total, reach, skew):
    if number_of == 2:
        one = jax.random.randint(rng, (), max(1, total - reach), min(reach, total - 1) + 1)
        return jnp.stack([one, total - one])
    sizes = jnp.asarray(length_profile(number_of, total, reach, skew), jnp.int32)
    couples = (number_of - 1) // 2
    giver, sink = sizes[1:1 + 2 * couples:2], sizes[2:2 + 2 * couples:2]
    room = jnp.minimum(giver - 1, reach - sink)
    passed = jax.random.randint(jax.random.fold_in(rng, 1), (couples,), 0, 1 << 20) % (room + 1)
    sizes = sizes.at[1:1 + 2 * couples:2].set(giver - passed).at[2:2 + 2 * couples:2].set(sink + passed)
    return sizes[jax.random.permutation(jax.random.fold_in(rng, 2), number_of)]


def normal_values(stream_key, extent, width, limit, shards=(), kind=jnp.bfloat16):
    gain = block_levels(stream_key, extent, shards, -0.22, 0.18) if shards else 1.0
    array = jax.random.normal(stream_key, extent, jnp.float32) * width * gain
    return jnp.minimum(jnp.maximum(array, -limit), limit).astype(kind)


def setup_inputs(seed: int = 0) -> dict:
    keys = jax.random.split(jax.random.key(seed), 9)
    return {
        "queries": draw_queries(jax.random.fold_in(keys[8], 71), 0),
        "key_rows": draw_key_rows(jax.random.fold_in(keys[8], 71), 0),
        "saved_value_rows": normal_values(keys[2], (BATCH_COUNT, SEQUENCE_LENGTH, KEY_HEADS * HEAD_SIZE), 1.0, 5.0, ((0, 4), (1, 32), (2, 2))),
        "out_grad": normal_values(keys[3], (BATCH_COUNT, SEQUENCE_LENGTH, QUERY_HEADS * HEAD_SIZE), 1.0, 5.0, ((0, 4), (1, 32), (2, 2))),
        "doc_lens": jax.vmap(lambda own: ragged_sizes(own, NDOC, SEQUENCE_LENGTH, SEQUENCE_LENGTH // 2, 2))(jax.random.split(keys[4], BATCH_COUNT)).reshape((BATCH_COUNT, NDOC)).astype(jnp.int32),
        "w_query": normal_values(keys[5], (MODEL_WIDTH, QUERY_HEADS * HEAD_SIZE), (QUERY_HEADS * HEAD_SIZE) ** -0.5, 0.125, ((0, 4), (1, 2))),
        "key_weight": normal_values(keys[6], (MODEL_WIDTH, KEY_HEADS * HEAD_SIZE), (KEY_HEADS * HEAD_SIZE) ** -0.5, 0.25, ((0, 4), (1, 2))),
        "value_weight": normal_values(keys[7], (MODEL_WIDTH, KEY_HEADS * HEAD_SIZE), (KEY_HEADS * HEAD_SIZE) ** -0.5, 0.25, ((0, 4), (1, 2))),
    }


negative_fill = -1.0e30


def segment_ids(lengths, positions):
    doc_ends = jnp.cumsum(lengths).astype(jnp.int32)
    return jnp.sum((positions[:, None] >= doc_ends[None, :-1]).astype(jnp.int32), axis=1)


def group_backward(operands, visible):
    query_group, key_block, value_block, grad_group = operands
    factor = HEAD_SIZE ** -0.5
    query_wide = query_group.astype(jnp.float32)
    key_wide = key_block.astype(jnp.float32)
    value_wide = value_block.astype(jnp.float32)
    grad_wide = grad_group.astype(jnp.float32)
    scores = jnp.einsum("hqd,kd->hqk", query_wide, key_wide) * factor
    masked = jnp.where(visible[None], scores, negative_fill)
    row_peak = jnp.max(masked, axis=-1, keepdims=True)
    row_total = jnp.sum(jnp.where(visible[None], jnp.exp(scores - row_peak), 0.0), axis=-1, keepdims=True)
    log_total = row_peak + jnp.log(row_total)
    weights = jnp.where(visible[None], jnp.exp(scores - log_total), 0.0).astype(jnp.bfloat16)
    weights_wide = lax.optimization_barrier(weights).astype(jnp.float32)
    outputs = jnp.einsum("hqk,kd->hqd", weights_wide, value_wide)
    row_delta = jnp.sum(grad_wide * outputs, axis=-1, keepdims=True)
    grad_scores = jnp.einsum("hqd,kd->hqk", grad_wide, value_wide)
    score_grads = (weights_wide * (grad_scores - row_delta)).astype(jnp.bfloat16)
    score_wide = lax.optimization_barrier(score_grads).astype(jnp.float32)
    query_grad = (jnp.einsum("hqk,kd->hqd", score_wide, key_wide) * factor).astype(jnp.bfloat16)
    key_gradient = (jnp.einsum("hqk,hqd->kd", score_wide, query_wide) * factor).astype(jnp.bfloat16)
    value_gradient = jnp.einsum("hqk,hqd->kd", weights_wide, grad_wide).astype(jnp.bfloat16)
    return query_grad, key_gradient, value_gradient


def reference(queries, key_rows, saved_value_rows, out_grad, doc_lens, w_query, key_weight, value_weight):
    def one_sequence(operands):
        query_sequence, key_sequence, value_sequence, gradient_sequence, lengths = operands
        positions = jnp.arange(SEQUENCE_LENGTH, dtype=jnp.int32)
        segments = segment_ids(lengths, positions)
        visible = (segments[:, None] == segments[None, :]) & (positions[None, :] <= positions[:, None])
        query_per_head = query_sequence.reshape(SEQUENCE_LENGTH, KEY_HEADS, QUERY_PER_KV, HEAD_SIZE).transpose(1, 2, 0, 3)
        gradient_per_head = gradient_sequence.reshape(SEQUENCE_LENGTH, KEY_HEADS, QUERY_PER_KV, HEAD_SIZE).transpose(1, 2, 0, 3)
        key_per_head = key_sequence.reshape(SEQUENCE_LENGTH, KEY_HEADS, HEAD_SIZE).transpose(1, 0, 2)
        value_per_head = value_sequence.reshape(SEQUENCE_LENGTH, KEY_HEADS, HEAD_SIZE).transpose(1, 0, 2)
        query_grad, key_gradient, value_gradient = lax.map(
            lambda operands_group: group_backward(operands_group, visible),
            (query_per_head, key_per_head, value_per_head, gradient_per_head))
        query_flat = query_grad.transpose(2, 0, 1, 3).reshape(SEQUENCE_LENGTH, QUERY_HEADS * HEAD_SIZE)
        key_flattened = key_gradient.transpose(1, 0, 2).reshape(SEQUENCE_LENGTH, KEY_HEADS * HEAD_SIZE)
        value_flattened = value_gradient.transpose(1, 0, 2).reshape(SEQUENCE_LENGTH, KEY_HEADS * HEAD_SIZE)
        summed = jnp.dot(query_flat, w_query.T, preferred_element_type=jnp.float32)
        summed = summed + jnp.dot(key_flattened, key_weight.T, preferred_element_type=jnp.float32)
        summed = summed + jnp.dot(value_flattened, value_weight.T, preferred_element_type=jnp.float32)
        return summed.astype(jnp.bfloat16)

    return lax.map(one_sequence, (queries, key_rows, saved_value_rows, out_grad, doc_lens))
```

```python
import functools

import jax
import jax.numpy as jnp
from jax import lax
from jax.experimental import pallas as pl
from jax.experimental.pallas import tpu as pltpu
from jax.sharding import PartitionSpec as P

HEAD = 128
GROUP = 4
ROWS = 128
CHUNK = 2 * ROWS
BACK = 4
CHUNKS = 2 * BACK + 1
FACTOR = HEAD**-0.5
FILL = -1e30
LOG2E = 1.4426950408889634
BF = jnp.bfloat16
F32 = jnp.float32


def nt(a, b):
    return lax.dot_general(a, b, (((1,), (1,)), ((), ())), preferred_element_type=F32)


def nn(a, b):
    return lax.dot_general(a, b, (((1,), (0,)), ((), ())), preferred_element_type=F32)


def tn(a, b):
    return lax.dot_general(a, b, (((0,), (0,)), ((), ())), preferred_element_type=F32)


def attention_kernel(info, qg0, qg1, *refs):
    own_in = refs[: BACK + 1]
    other_in = refs[BACK + 1]
    dq0, dq1, own_out, other_out = refs[BACK + 2 : BACK + 6]
    kv, s_buf, p_buf, part, q_all, g_all = refs[BACK + 6 :]
    block_base, core, odd = info[0], info[1], info[2]
    for n in range(BACK + 1):
        kv[n] = own_in[n][...]
    for n in range(BACK):
        kv[BACK + 1 + n] = other_in[n]
    for h in range(GROUP):
        for slot, ref in enumerate((qg0, qg1)):
            q_all[h, slot * ROWS : (slot + 1) * ROWS, :] = ref[:, h * HEAD : (h + 1) * HEAD]
            g_all[h, slot * ROWS : (slot + 1) * ROWS, :] = ref[
                :, (GROUP + h) * HEAD : (GROUP + h + 1) * HEAD
            ]

    lane = lax.broadcasted_iota(jnp.int32, (1, CHUNK), 1)
    query_pos = block_base + core * CHUNK + jnp.bitwise_xor(lane, odd * ROWS)
    doc_first = jnp.zeros_like(query_pos)
    end = info[8]
    for d in range(7):
        if d:
            end = end + info[8 + d]
        doc_first = jnp.where(query_pos >= end, end, doc_first)
    key_row = jnp.bitwise_xor(
        lax.broadcasted_iota(jnp.int32, (CHUNK, CHUNK), 0), odd * ROWS
    )

    def chunk_base(n):
        own = block_base - n * 2 * CHUNK + core * CHUNK
        i = n - (BACK + 1)
        other = jnp.where(core == 0, block_base - (i + 1) * 2 * CHUNK + CHUNK, block_base - i * 2 * CHUNK)
        return jnp.where(n <= BACK, own, other)

    def score_step(n, peak):
        base = chunk_base(n)
        visible = (key_row >= doc_first - base) & (key_row <= query_pos - base)
        keys = kv[n, :, :HEAD]
        out = []
        for h in range(GROUP):
            s = jnp.where(visible, nt(keys, q_all[h]), FILL)
            s_buf[n, h] = s
            out.append(jnp.maximum(peak[h], jnp.max(s.reshape(CHUNK // 8, 8, CHUNK), axis=0)))
        return tuple(out)

    peak = lax.fori_loop(
        0, CHUNKS, score_step, tuple(jnp.full((8, CHUNK), FILL, F32) for _ in range(GROUP))
    )
    peak = [jnp.max(m, axis=0, keepdims=True) for m in peak]

    def weight_step(n, carry):
        totals, deltas = carry
        values = kv[n, :, HEAD:]
        new_t, new_d = [], []
        for h in range(GROUP):
            e = jnp.exp2((s_buf[n, h] - peak[h]) * (FACTOR * LOG2E))
            dp = nt(values, g_all[h])
            s_buf[n, h] = e
            p_buf[n, h] = dp
            new_t.append(totals[h] + jnp.sum(e.reshape(CHUNK // 8, 8, CHUNK), axis=0))
            new_d.append(deltas[h] + jnp.sum((e * dp).reshape(CHUNK // 8, 8, CHUNK), axis=0))
        return tuple(new_t), tuple(new_d)

    zero = tuple(jnp.zeros((8, CHUNK), F32) for _ in range(GROUP))
    totals, deltas = lax.fori_loop(0, CHUNKS, weight_step, (zero, zero))
    inverse = [1.0 / jnp.sum(t, axis=0, keepdims=True) for t in totals]
    delta = [jnp.sum(d, axis=0, keepdims=True) * inverse[h] for h, d in enumerate(deltas)]

    def grad_step(n, acc):
        keys = kv[n, :, :HEAD]
        dk = jnp.zeros((CHUNK, HEAD), F32)
        dv = jnp.zeros((CHUNK, HEAD), F32)
        out = []
        for h in range(GROUP):
            w = s_buf[n, h] * inverse[h]
            ds = (w * (p_buf[n, h] - delta[h])).astype(BF)
            w = w.astype(BF)
            dv = dv + nn(w, g_all[h])
            dk = dk + nn(ds, q_all[h])
            out.append(acc[h] + tn(keys, ds))
        part[n, :, :HEAD] = dk * FACTOR
        part[n, :, HEAD:] = dv
        return tuple(out)

    acc = lax.fori_loop(
        0, CHUNKS, grad_step, tuple(jnp.zeros((HEAD, CHUNK), F32) for _ in range(GROUP))
    )
    for h in range(GROUP):
        g = (jnp.transpose(acc[h]) * FACTOR).astype(BF)
        dq0[:, h * HEAD : (h + 1) * HEAD] = g[:ROWS]
        dq1[:, h * HEAD : (h + 1) * HEAD] = g[ROWS:]
    for n in range(BACK + 1):
        own_out[n] = part[n]
    for n in range(BACK):
        other_out[n] = part[BACK + 1 + n].astype(BF)


def attention(info, qg0, qg1, own_blocks, other_blocks):
    vmem = pl.BlockSpec(memory_space=pltpu.VMEM)
    return pl.pallas_call(
        attention_kernel,
        out_shape=(
            jax.ShapeDtypeStruct((ROWS, GROUP * HEAD), BF),
            jax.ShapeDtypeStruct((ROWS, GROUP * HEAD), BF),
            jax.ShapeDtypeStruct((BACK + 1, CHUNK, 2 * HEAD), F32),
            jax.ShapeDtypeStruct((BACK, CHUNK, 2 * HEAD), BF),
        ),
        in_specs=[pl.BlockSpec(memory_space=pltpu.SMEM)] + [vmem] * (BACK + 4),
        out_specs=(vmem,) * 4,
        scratch_shapes=[
            pltpu.VMEM((CHUNKS, CHUNK, 2 * HEAD), BF),
            pltpu.VMEM((CHUNKS, GROUP, CHUNK, CHUNK), F32),
            pltpu.VMEM((CHUNKS, GROUP, CHUNK, CHUNK), F32),
            pltpu.VMEM((CHUNKS, CHUNK, 2 * HEAD), F32),
            pltpu.VMEM((GROUP, CHUNK, HEAD), BF),
            pltpu.VMEM((GROUP, CHUNK, HEAD), BF),
        ],
        compiler_params=pltpu.CompilerParams(vmem_limit_bytes=40 * 1024 * 1024),
        cost_estimate=pl.CostEstimate(
            flops=5 * 2 * CHUNKS * GROUP * CHUNK * CHUNK * HEAD,
            bytes_accessed=8 << 20,
            transcendentals=CHUNKS * GROUP * CHUNK * CHUNK,
        ),
        name="attention_grads",
    )(info, qg0, qg1, *own_blocks, other_blocks)


def body(queries, key_rows, saved_value_rows, out_grad, doc_lens, w_query, key_weight, value_weight):
    servers = lax.axis_size("server")
    dps = lax.axis_size("dp")
    server = lax.axis_index("server")
    core = lax.axis_index("section")
    dp = lax.axis_index("dp")
    odd = server % 2
    both = ("server", "section")

    def swap_pairs(j):
        pairs = []
        for s in range(servers):
            z, a, b = s // 4, (s % 4) // 2, s % 2
            for c in range(2):
                target = z * 4 + 2 * c + (b ^ j)
                pairs.append((2 * s + c, 2 * target + a))
        return pairs

    pairs = [swap_pairs(0), swap_pairs(1)]

    def swap(x, j):
        return lax.ppermute(x, both, pairs[j])

    def shift(x, axis, k):
        n = lax.axis_size(axis)
        return lax.ppermute(x, axis, [(i, (i + k) % n) for i in range(n)])

    def flip(x):
        return lax.ppermute(x, "section", [(0, 1), (1, 0)])

    def groups(left, right):
        half = left.shape[-1] // 2
        first = jnp.concatenate([left[:, :half], right[:, :half]], 1)
        second = jnp.concatenate([left[:, half:], right[:, half:]], 1)
        return jnp.where(odd == 0, first, second), jnp.where(odd == 0, second, first)

    kv_first, kv_second = groups(key_rows[0], saved_value_rows[0])
    block = jnp.concatenate([swap(kv_first, 0), swap(kv_second, 1)], 0)
    qg_first, qg_second = groups(queries[0], out_grad[0])
    qg0, qg1 = swap(qg_first, 0), swap(qg_second, 1)

    blocks = [block]
    for _ in range(BACK):
        blocks.append(shift(blocks[-1], "server", 4))
    low = jnp.stack(blocks[:BACK])
    high = jnp.stack(blocks[1:])
    other = flip(jnp.where(core == 0, low, high))

    info = jnp.concatenate(
        [
            jnp.stack([(server // 4) * (4 * ROWS), core, odd]).astype(jnp.int32),
            jnp.zeros((5,), jnp.int32),
            doc_lens[0].astype(jnp.int32),
        ]
    )
    dq0, dq1, own_part, other_part = attention(info, qg0, qg1, blocks, other)

    def my_columns(w):
        half = w.shape[0] // 2
        mine = jnp.where(core == 0, w[:half], w[half:])
        theirs = jnp.where(core == 0, w[half:], w[:half])
        return mine, flip(theirs)

    kw_first, kw_second = groups(key_weight, value_weight)
    kv_weight = jnp.concatenate(my_columns(jnp.concatenate([kw_first, kw_second], 1)), 1)
    kv_weight = lax.all_gather(kv_weight, "dp", axis=0, tiled=True)
    half = w_query.shape[1] // 2
    wq = jnp.where(odd == 0, w_query, jnp.concatenate([w_query[:, half:], w_query[:, :half]], 1))
    wq_mine, wq_theirs = my_columns(wq)

    dq = jnp.concatenate([swap(dq0, 0), swap(dq1, 1)], 1)
    rows = jnp.concatenate([dq] + [shift(dq, "dp", k) for k in range(1, dps)], 0)
    projected = (nt(rows, wq_mine) + nt(flip(rows), wq_theirs)).astype(BF)
    columns = [projected[:ROWS]] + [
        shift(projected[k * ROWS : (k + 1) * ROWS], "dp", -k) for k in range(1, dps)
    ]
    columns = jnp.stack(columns + columns)
    query_term = lax.dynamic_slice_in_dim(columns, (dps - dp) % dps, dps, 0)

    arrived = flip(other_part)
    zero = jnp.zeros_like(arrived[0])
    held = None
    for k in range(BACK, -1, -1):
        total = own_part[k] + jnp.where(
            core == 0, arrived[k] if k < BACK else zero, arrived[k - 1] if k else zero
        ).astype(F32)
        if held is not None:
            total = total + shift(held, "server", -4).astype(F32)
        held = total.astype(BF)
    kv_grad = jnp.concatenate([swap(held[:ROWS], 0), swap(held[ROWS:], 1)], 1)
    kv_grad = jnp.concatenate([kv_grad, flip(kv_grad)], 1)
    kv_term = nt(kv_grad, kv_weight)
    mine = kv_term.reshape(ROWS, dps, -1) + query_term.transpose(1, 0, 2).astype(F32)
    mine = mine.astype(BF)
    theirs = flip(mine)
    out = jnp.stack(
        [jnp.where(core == 0, mine, theirs), jnp.where(core == 0, theirs, mine)], 2
    )
    return out.reshape(1, ROWS, -1)


def solution(mesh):
    return jax.shard_map(
        body,
        mesh=mesh,
        in_specs=(
            P("dp", "server", "section"),
            P("dp", "server", "section"),
            P("dp", "server", "section"),
            P("dp", "server", "section"),
            P("dp", None),
            P("dp", "section"),
            P("dp", "section"),
            P("dp", "section"),
        ),
        out_specs=P("dp", "server", None),
        check_vma=False,
    )
```

```python
import functools

import jax
import jax.numpy as jnp
from jax import lax
from jax.experimental import pallas as pl
from jax.experimental.pallas import tpu as pltpu
from jax.sharding import PartitionSpec as P

HEAD = 128
GROUP = 4
ROWS = 128
CHUNK = 2 * ROWS
BACK = 4
CHUNKS = 2 * BACK + 1
FACTOR = HEAD**-0.5
FILL = -1e30
LOG2E = 1.4426950408889634
BF = jnp.bfloat16
F32 = jnp.float32


def nt(a, b):
    return lax.dot_general(a, b, (((1,), (1,)), ((), ())), preferred_element_type=F32)


def nn(a, b):
    return lax.dot_general(a, b, (((1,), (0,)), ((), ())), preferred_element_type=F32)


def tn(a, b):
    return lax.dot_general(a, b, (((0,), (0,)), ((), ())), preferred_element_type=F32)


def attention_kernel(info, qg0, qg1, *refs):
    own_in = refs[: BACK + 1]
    other_in = refs[BACK + 1]
    dq, own_out, other_out, kv, s_buf, p_buf, part, q_all, g_all = refs[-9:]
    block_base, core, odd = info[0], info[1], info[2]
    for n in range(BACK + 1):
        kv[n] = own_in[n][...]
    for n in range(BACK):
        kv[BACK + 1 + n] = other_in[n]
    for h in range(GROUP):
        for slot, ref in enumerate((qg0, qg1)):
            q_all[h, slot * ROWS : (slot + 1) * ROWS, :] = ref[:, h * HEAD : (h + 1) * HEAD]
            g_all[h, slot * ROWS : (slot + 1) * ROWS, :] = ref[
                :, (GROUP + h) * HEAD : (GROUP + h + 1) * HEAD
            ]

    lane = lax.broadcasted_iota(jnp.int32, (1, CHUNK), 1)
    query_pos = block_base + core * CHUNK + jnp.bitwise_xor(lane, odd * ROWS)
    doc_first = jnp.zeros_like(query_pos)
    end = info[8]
    for d in range(7):
        if d:
            end = end + info[8 + d]
        doc_first = jnp.where(query_pos >= end, end, doc_first)
    key_row = jnp.bitwise_xor(
        lax.broadcasted_iota(jnp.int32, (CHUNK, CHUNK), 0), odd * ROWS
    )

    def chunk_base(n):
        own = block_base - n * 2 * CHUNK + core * CHUNK
        i = n - (BACK + 1)
        other = jnp.where(core == 0, block_base - (i + 1) * 2 * CHUNK + CHUNK, block_base - i * 2 * CHUNK)
        return jnp.where(n <= BACK, own, other)

    def score_step(n, peak):
        base = chunk_base(n)
        visible = (key_row >= doc_first - base) & (key_row <= query_pos - base)
        keys = kv[n, :, :HEAD]
        out = []
        for h in range(GROUP):
            s = jnp.where(visible, nt(keys, q_all[h]), FILL)
            s_buf[n, h] = s
            out.append(jnp.maximum(peak[h], jnp.max(s.reshape(CHUNK // 8, 8, CHUNK), axis=0)))
        return tuple(out)

    peak = lax.fori_loop(
        0, CHUNKS, score_step, tuple(jnp.full((8, CHUNK), FILL, F32) for _ in range(GROUP))
    )
    peak = [jnp.max(m, axis=0, keepdims=True) for m in peak]

    def weight_step(n, carry):
        totals, deltas = carry
        values = kv[n, :, HEAD:]
        new_t, new_d = [], []
        for h in range(GROUP):
            e = jnp.exp2((s_buf[n, h] - peak[h]) * (FACTOR * LOG2E))
            dp = nt(values, g_all[h])
            s_buf[n, h] = e
            p_buf[n, h] = dp
            new_t.append(totals[h] + jnp.sum(e.reshape(CHUNK // 8, 8, CHUNK), axis=0))
            new_d.append(deltas[h] + jnp.sum((e * dp).reshape(CHUNK // 8, 8, CHUNK), axis=0))
        return tuple(new_t), tuple(new_d)

    zero = tuple(jnp.zeros((8, CHUNK), F32) for _ in range(GROUP))
    totals, deltas = lax.fori_loop(0, CHUNKS, weight_step, (zero, zero))
    inverse = [1.0 / jnp.sum(t, axis=0, keepdims=True) for t in totals]
    delta = [jnp.sum(d, axis=0, keepdims=True) * inverse[h] for h, d in enumerate(deltas)]

    def grad_step(n, acc):
        keys = kv[n, :, :HEAD]
        dk = jnp.zeros((CHUNK, HEAD), F32)
        dv = jnp.zeros((CHUNK, HEAD), F32)
        out = []
        for h in range(GROUP):
            w = s_buf[n, h] * inverse[h]
            ds = (w * (p_buf[n, h] - delta[h])).astype(BF)
            w = w.astype(BF)
            dv = dv + nn(w, g_all[h])
            dk = dk + nn(ds, q_all[h])
            out.append(acc[h] + tn(keys, ds))
        part[n, :, :HEAD] = dk * FACTOR
        part[n, :, HEAD:] = dv
        return tuple(out)

    acc = lax.fori_loop(
        0, CHUNKS, grad_step, tuple(jnp.zeros((HEAD, CHUNK), F32) for _ in range(GROUP))
    )
    for h in range(GROUP):
        dq[:, h * HEAD : (h + 1) * HEAD] = (jnp.transpose(acc[h]) * FACTOR).astype(BF)
    for n in range(BACK + 1):
        own_out[n] = part[n]
    for n in range(BACK):
        other_out[n] = part[BACK + 1 + n].astype(BF)


def attention(info, qg0, qg1, own_blocks, other_blocks, after):
    vmem = pl.BlockSpec(memory_space=pltpu.VMEM)
    return pl.pallas_call(
        attention_kernel,
        out_shape=(
            jax.ShapeDtypeStruct((CHUNK, GROUP * HEAD), BF),
            jax.ShapeDtypeStruct((BACK + 1, CHUNK, 2 * HEAD), F32),
            jax.ShapeDtypeStruct((BACK, CHUNK, 2 * HEAD), BF),
        ),
        in_specs=[pl.BlockSpec(memory_space=pltpu.SMEM)]
        + [vmem] * (BACK + 4)
        + [pl.BlockSpec(memory_space=pl.ANY)] * len(after),
        out_specs=(vmem,) * 3,
        scratch_shapes=[
            pltpu.VMEM((CHUNKS, CHUNK, 2 * HEAD), BF),
            pltpu.VMEM((CHUNKS, GROUP, CHUNK, CHUNK), F32),
            pltpu.VMEM((CHUNKS, GROUP, CHUNK, CHUNK), F32),
            pltpu.VMEM((CHUNKS, CHUNK, 2 * HEAD), F32),
            pltpu.VMEM((GROUP, CHUNK, HEAD), BF),
            pltpu.VMEM((GROUP, CHUNK, HEAD), BF),
        ],
        compiler_params=pltpu.CompilerParams(vmem_limit_bytes=30 * 1024 * 1024),
        cost_estimate=pl.CostEstimate(
            flops=5 * 2 * CHUNKS * GROUP * CHUNK * CHUNK * HEAD,
            bytes_accessed=8 << 20,
            transcendentals=CHUNKS * GROUP * CHUNK * CHUNK,
        ),
        name="attention_grads",
    )(info, qg0, qg1, *own_blocks, other_blocks, *after)


def project_query_kernel(info, dq, other, *refs):
    n = (len(refs) - 1) // 2
    weights, outs, rows = refs[:n], refs[n : 2 * n], refs[2 * n]
    core, odd, chip = info[1], info[2], info[3]
    for source, c in ((dq, core), (other, 1 - core)):
        for slot in range(2):
            owner = 2 * c + jnp.bitwise_xor(odd, slot)
            at = pl.multiple_of(lax.rem(owner - chip + 4, 4) * ROWS, ROWS)
            rows[pl.ds(at, ROWS), :] = source[slot * ROWS : (slot + 1) * ROWS, :]
    for k in range(n):
        width = weights[k].shape[0]
        product = nt(rows[...], weights[k][...]).astype(BF)
        for i in range(4):
            outs[i][:, k * width : (k + 1) * width] = product[i * ROWS : (i + 1) * ROWS]


def project_query(info, dq, other, weights):
    vmem = pl.BlockSpec(memory_space=pltpu.VMEM)
    n, width, dims = len(weights), weights[0].shape[0], dq.shape[1]
    return pl.pallas_call(
        project_query_kernel,
        grid=(1,),
        out_shape=(jax.ShapeDtypeStruct((ROWS, n * width), BF),) * 4,
        in_specs=[pl.BlockSpec(memory_space=pltpu.SMEM), vmem, vmem]
        + [pl.BlockSpec((width, dims), lambda i, at=w.shape[1] // dims - 1: (0, at)) for w in weights],
        out_specs=(vmem,) * 4,
        scratch_shapes=[pltpu.VMEM((4 * ROWS, dims), BF)],
        compiler_params=pltpu.CompilerParams(vmem_limit_bytes=24 * 1024 * 1024),
        cost_estimate=pl.CostEstimate(
            flops=8 * ROWS * n * width * dims, bytes_accessed=4 << 20, transcendentals=0
        ),
        name="project_query",
    )(info, dq, other, *weights)


def project_kernel(grad, *refs):
    n = len(refs) - 5
    out = refs[-1]
    for k in range(n):
        width = refs[k].shape[0]
        total = nt(grad[...], refs[k][...])
        for term in refs[n : n + 4]:
            total = total + term[:, k * width : (k + 1) * width].astype(F32)
        out[k] = total.astype(BF)


def project(grad, weights, terms):
    vmem = pl.BlockSpec(memory_space=pltpu.VMEM)
    n, width, dims = len(weights), weights[0].shape[0], grad.shape[1]
    return pl.pallas_call(
        project_kernel,
        grid=(1,),
        out_shape=jax.ShapeDtypeStruct((n, ROWS, width), BF),
        in_specs=[vmem] + [pl.BlockSpec((width, dims), lambda i: (0, 0))] * n + [vmem] * 4,
        out_specs=vmem,
        compiler_params=pltpu.CompilerParams(vmem_limit_bytes=24 * 1024 * 1024),
        cost_estimate=pl.CostEstimate(
            flops=2 * n * ROWS * width * dims, bytes_accessed=8 << 20, transcendentals=0
        ),
        name="project_kv",
    )(grad, *weights, *terms)


def assemble_kernel(where, mine, theirs, out):
    n, _, width = mine.shape
    for k in range(n):
        piece = lax.rem(where[0] - k + n, n) * 2
        near = pl.multiple_of((piece + where[1]) * width, width)
        far = pl.multiple_of((piece + 1 - where[1]) * width, width)
        out[:, pl.ds(near, width)] = mine[k]
        out[:, pl.ds(far, width)] = theirs[k]


def assemble(where, mine, theirs):
    vmem = pl.BlockSpec(memory_space=pltpu.VMEM)
    n, rows, width = mine.shape
    return pl.pallas_call(
        assemble_kernel,
        out_shape=jax.ShapeDtypeStruct((rows, 2 * n * width), BF),
        in_specs=[pl.BlockSpec(memory_space=pltpu.SMEM), vmem, vmem],
        out_specs=vmem,
        compiler_params=pltpu.CompilerParams(vmem_limit_bytes=16 * 1024 * 1024),
        name="assemble",
    )(where, mine, theirs)


def body(queries, key_rows, saved_value_rows, out_grad, doc_lens, w_query, key_weight, value_weight):
    servers = lax.axis_size("server")
    dps = lax.axis_size("dp")
    server = lax.axis_index("server")
    core = lax.axis_index("section")
    dp = lax.axis_index("dp")
    odd = server % 2
    both = ("server", "section")

    def swap_pairs(j):
        pairs = []
        for s in range(servers):
            z, a, b = s // 4, (s % 4) // 2, s % 2
            for c in range(2):
                target = z * 4 + 2 * c + (b ^ j)
                pairs.append((2 * s + c, 2 * target + a))
        return pairs

    pairs = [swap_pairs(0), swap_pairs(1)]

    def swap(x, j):
        return lax.ppermute(x, both, pairs[j])

    def shift(x, axis, k):
        n = lax.axis_size(axis)
        return lax.ppermute(x, axis, [(i, (i + k) % n) for i in range(n)])

    def flip(x):
        return lax.ppermute(x, "section", [(0, 1), (1, 0)])

    def groups(left, right):
        half = left.shape[-1] // 2
        first = jnp.concatenate([left[:, :half], right[:, :half]], 1)
        second = jnp.concatenate([left[:, half:], right[:, half:]], 1)
        return jnp.where(odd == 0, first, second), jnp.where(odd == 0, second, first)

    kv_first, kv_second = groups(key_rows[0], saved_value_rows[0])
    block = jnp.concatenate([swap(kv_first, 0), swap(kv_second, 1)], 0)
    blocks = [block]
    for _ in range(BACK):
        blocks.append(shift(blocks[-1], "server", 4))

    queries, out_grad, _ = lax.optimization_barrier((queries, out_grad, block))
    qg_first, qg_second = groups(queries[0], out_grad[0])
    qg0, qg1 = swap(qg_first, 0), swap(qg_second, 1)

    kw_first, kw_second = groups(key_weight, value_weight)
    half = w_query.shape[1] // 2
    weight = jnp.concatenate(
        [kw_first, kw_second, jnp.where(odd == 0, w_query[:, :half], w_query[:, half:])], 1
    )
    half = weight.shape[0] // 2
    mine = jnp.where(core == 0, weight[:half], weight[half:])
    theirs = flip(jnp.where(core == 0, weight[half:], weight[:half]))
    half = 2 * kw_first.shape[1]
    wide = jnp.concatenate(
        [
            mine[:, :half],
            theirs[:, :half],
            jnp.where(core == (server % 4) // 2, mine[:, half:], theirs[:, half:]),
        ],
        1,
    )
    early = {k: shift(wide if k != 2 else wide[:, 2 * half :], "dp", k) for k in range(1, dps)}

    low = jnp.stack(blocks[:BACK])
    high = jnp.stack(blocks[1:])
    other = flip(jnp.where(core == 0, low, high))

    info = jnp.concatenate(
        [
            jnp.stack([(server // 4) * (4 * ROWS), core, odd, server % 4]).astype(jnp.int32),
            jnp.zeros((4,), jnp.int32),
            doc_lens[0].astype(jnp.int32),
        ]
    )
    dq, own_part, other_part = attention(
        info, qg0, qg1, blocks, other, [early[k] for k in early if k != 2]
    )

    arrived = flip(other_part)
    zero = jnp.zeros_like(arrived[:1])
    arrived = jnp.where(
        core == 0,
        jnp.concatenate([arrived, zero], 0),
        jnp.concatenate([zero, arrived], 0),
    )
    totals = own_part + arrived.astype(F32)
    held = totals[BACK].astype(BF)

    early[0] = wide
    late = dict(early)
    late[2] = shift(wide[:, : 2 * half], "dp", 2)
    early, late = [[w[k] for k in range(dps)] for w in (early, late)]

    sent_products = project_query(info, dq, flip(dq), early)
    products = [sent_products[0]]
    for k in range(1, 4):
        pairs_x = [(s, s // 4 * 4 + (s + k) % 4) for s in range(servers)]
        products.append(lax.ppermute(sent_products[k], "server", pairs_x))

    for k in range(BACK - 1, -1, -1):
        held = (totals[k] + shift(held, "server", -4).astype(F32)).astype(BF)
    held, products = lax.optimization_barrier((held, products))
    kv_grad = jnp.concatenate([swap(held[:ROWS], 0), swap(held[ROWS:], 1)], 1)
    kv_grad = jnp.concatenate([kv_grad, flip(kv_grad)], 1)
    mine = project(kv_grad, late, products)
    theirs = flip(mine)
    where = jnp.stack([dp, core]).astype(jnp.int32)
    return assemble(where, mine, theirs)[None]


def solution(mesh):
    return jax.shard_map(
        body,
        mesh=mesh,
        in_specs=(
            P("dp", "server", "section"),
            P("dp", "server", "section"),
            P("dp", "server", "section"),
            P("dp", "server", "section"),
            P("dp", None),
            P("dp", "section"),
            P("dp", "section"),
            P("dp", "section"),
        ),
        out_specs=P("dp", "server", None),
        check_vma=False,
    )
```

```python
import functools

import jax
import jax.numpy as jnp
from jax import lax
from jax.experimental import pallas as pl
from jax.experimental.pallas import tpu as pltpu
from jax.sharding import PartitionSpec as P

HEAD = 128
GROUP = 4
ROWS = 128
CHUNK = 2 * ROWS
BACK = 4
CHUNKS = 2 * BACK + 1
FACTOR = HEAD**-0.5
FILL = -1e30
LOG2E = 1.4426950408889634
BF = jnp.bfloat16
F32 = jnp.float32


def nt(a, b):
    return lax.dot_general(a, b, (((1,), (1,)), ((), ())), preferred_element_type=F32)


def nn(a, b):
    return lax.dot_general(a, b, (((1,), (0,)), ((), ())), preferred_element_type=F32)


def tn(a, b):
    return lax.dot_general(a, b, (((0,), (0,)), ((), ())), preferred_element_type=F32)


def attention_kernel(info, qg0, qg1, *refs):
    own_in = refs[: BACK + 1]
    other_in = refs[BACK + 1]
    dq, own_out, other_out, kv, s_buf, p_buf, part, q_all, g_all = refs[-9:]
    block_base, core, odd = info[0], info[1], info[2]
    for n in range(BACK + 1):
        kv[n] = own_in[n][...]
    for n in range(BACK):
        kv[BACK + 1 + n] = other_in[n]
    for h in range(GROUP):
        for slot, ref in enumerate((qg0, qg1)):
            q_all[h, slot * ROWS : (slot + 1) * ROWS, :] = ref[:, h * HEAD : (h + 1) * HEAD]
            g_all[h, slot * ROWS : (slot + 1) * ROWS, :] = ref[
                :, (GROUP + h) * HEAD : (GROUP + h + 1) * HEAD
            ]

    lane = lax.broadcasted_iota(jnp.int32, (1, CHUNK), 1)
    query_pos = block_base + core * CHUNK + jnp.bitwise_xor(lane, odd * ROWS)
    doc_first = jnp.zeros_like(query_pos)
    end = info[8]
    for d in range(7):
        if d:
            end = end + info[8 + d]
        doc_first = jnp.where(query_pos >= end, end, doc_first)
    key_row = jnp.bitwise_xor(
        lax.broadcasted_iota(jnp.int32, (CHUNK, CHUNK), 0), odd * ROWS
    )

    def chunk_base(n):
        own = block_base - n * 2 * CHUNK + core * CHUNK
        i = n - (BACK + 1)
        other = jnp.where(core == 0, block_base - (i + 1) * 2 * CHUNK + CHUNK, block_base - i * 2 * CHUNK)
        return jnp.where(n <= BACK, own, other)

    def score_step(n, peak):
        base = chunk_base(n)
        visible = (key_row >= doc_first - base) & (key_row <= query_pos - base)
        keys = kv[n, :, :HEAD]
        out = []
        for h in range(GROUP):
            s = jnp.where(visible, nt(keys, q_all[h]), FILL)
            s_buf[n, h] = s
            out.append(jnp.maximum(peak[h], jnp.max(s.reshape(CHUNK // 8, 8, CHUNK), axis=0)))
        return tuple(out)

    peak = lax.fori_loop(
        0, CHUNKS, score_step, tuple(jnp.full((8, CHUNK), FILL, F32) for _ in range(GROUP))
    )
    peak = [jnp.max(m, axis=0, keepdims=True) for m in peak]

    def weight_step(n, carry):
        totals, deltas = carry
        values = kv[n, :, HEAD:]
        new_t, new_d = [], []
        for h in range(GROUP):
            e = jnp.exp2((s_buf[n, h] - peak[h]) * (FACTOR * LOG2E))
            dp = nt(values, g_all[h])
            s_buf[n, h] = e
            p_buf[n, h] = dp
            new_t.append(totals[h] + jnp.sum(e.reshape(CHUNK // 8, 8, CHUNK), axis=0))
            new_d.append(deltas[h] + jnp.sum((e * dp).reshape(CHUNK // 8, 8, CHUNK), axis=0))
        return tuple(new_t), tuple(new_d)

    zero = tuple(jnp.zeros((8, CHUNK), F32) for _ in range(GROUP))
    totals, deltas = lax.fori_loop(0, CHUNKS, weight_step, (zero, zero))
    inverse = [1.0 / jnp.sum(t, axis=0, keepdims=True) for t in totals]
    delta = [jnp.sum(d, axis=0, keepdims=True) * inverse[h] for h, d in enumerate(deltas)]

    def grad_step(n, acc):
        keys = kv[n, :, :HEAD]
        dk = jnp.zeros((CHUNK, HEAD), F32)
        dv = jnp.zeros((CHUNK, HEAD), F32)
        out = []
        for h in range(GROUP):
            w = s_buf[n, h] * inverse[h]
            ds = (w * (p_buf[n, h] - delta[h])).astype(BF)
            w = w.astype(BF)
            dv = dv + nn(w, g_all[h])
            dk = dk + nn(ds, q_all[h])
            out.append(acc[h] + tn(keys, ds))
        part[n, :, :HEAD] = dk * FACTOR
        part[n, :, HEAD:] = dv
        return tuple(out)

    acc = lax.fori_loop(
        0, CHUNKS, grad_step, tuple(jnp.zeros((HEAD, CHUNK), F32) for _ in range(GROUP))
    )
    for h in range(GROUP):
        dq[:, h * HEAD : (h + 1) * HEAD] = (jnp.transpose(acc[h]) * FACTOR).astype(BF)
    for n in range(BACK + 1):
        own_out[n] = part[n]
    for n in range(BACK):
        other_out[n] = part[BACK + 1 + n].astype(BF)


def attention(info, qg0, qg1, own_blocks, other_blocks, after):
    vmem = pl.BlockSpec(memory_space=pltpu.VMEM)
    return pl.pallas_call(
        attention_kernel,
        out_shape=(
            jax.ShapeDtypeStruct((CHUNK, GROUP * HEAD), BF),
            jax.ShapeDtypeStruct((BACK + 1, CHUNK, 2 * HEAD), F32),
            jax.ShapeDtypeStruct((BACK, CHUNK, 2 * HEAD), BF),
        ),
        in_specs=[pl.BlockSpec(memory_space=pltpu.SMEM)]
        + [vmem] * (BACK + 4)
        + [pl.BlockSpec(memory_space=pl.ANY)] * len(after),
        out_specs=(vmem,) * 3,
        scratch_shapes=[
            pltpu.VMEM((CHUNKS, CHUNK, 2 * HEAD), BF),
            pltpu.VMEM((CHUNKS, GROUP, CHUNK, CHUNK), F32),
            pltpu.VMEM((CHUNKS, GROUP, CHUNK, CHUNK), F32),
            pltpu.VMEM((CHUNKS, CHUNK, 2 * HEAD), F32),
            pltpu.VMEM((GROUP, CHUNK, HEAD), BF),
            pltpu.VMEM((GROUP, CHUNK, HEAD), BF),
        ],
        compiler_params=pltpu.CompilerParams(vmem_limit_bytes=30 * 1024 * 1024),
        cost_estimate=pl.CostEstimate(
            flops=5 * 2 * CHUNKS * GROUP * CHUNK * CHUNK * HEAD,
            bytes_accessed=8 << 20,
            transcendentals=CHUNKS * GROUP * CHUNK * CHUNK,
        ),
        name="attention_grads",
    )(info, qg0, qg1, *own_blocks, other_blocks, *after)


def project_query_kernel(info, own, arrived, dq, other, *refs):
    weights, *outs, totals, held, rows = refs
    core, odd, chip = info[1], info[2], info[3]
    for k in range(BACK + 1):
        near = arrived[k].astype(F32) if k < BACK else 0.0
        far = arrived[k - 1].astype(F32) if k else 0.0
        total = own[k] + jnp.where(core == 0, near, far)
        if k < BACK:
            totals[k] = total
        else:
            held[...] = total.astype(BF)
    for source, c in ((dq, core), (other, 1 - core)):
        for slot in range(2):
            owner = 2 * c + jnp.bitwise_xor(odd, slot)
            at = pl.multiple_of(lax.rem(owner - chip + 4, 4) * ROWS, ROWS)
            rows[pl.ds(at, ROWS), :] = source[slot * ROWS : (slot + 1) * ROWS, :]
    width = 4 * ROWS
    for k in range(weights.shape[0] // width):
        product = nt(rows[...], weights[k * width : (k + 1) * width]).astype(BF)
        for i in range(4):
            outs[i][:, k * width : (k + 1) * width] = product[i * ROWS : (i + 1) * ROWS]


def project_query(info, own, arrived, dq, other, weights):
    vmem = pl.BlockSpec(memory_space=pltpu.VMEM)
    width, dims = weights.shape
    return pl.pallas_call(
        project_query_kernel,
        out_shape=(jax.ShapeDtypeStruct((ROWS, width), BF),) * 4
        + (
            jax.ShapeDtypeStruct((BACK,) + own.shape[1:], F32),
            jax.ShapeDtypeStruct(own.shape[1:], BF),
        ),
        in_specs=[pl.BlockSpec(memory_space=pltpu.SMEM)]
        + [vmem] * 5,
        out_specs=(vmem,) * 6,
        scratch_shapes=[pltpu.VMEM((4 * ROWS, dims), BF)],
        compiler_params=pltpu.CompilerParams(vmem_limit_bytes=24 * 1024 * 1024),
        cost_estimate=pl.CostEstimate(
            flops=8 * ROWS * width * dims, bytes_accessed=4 << 20, transcendentals=0
        ),
        name="project_query",
    )(info, own, arrived, dq, other, weights)


def project_kernel(grad, weights, *refs):
    *terms, out = refs
    n, _, width = out.shape
    for k in range(n):
        at = slice(k * width, (k + 1) * width)
        total = nt(grad[...], weights[at])
        for term in terms:
            total = total + term[:, at].astype(F32)
        out[k] = total.astype(BF)


def project(grad, weights, terms, n):
    vmem = pl.BlockSpec(memory_space=pltpu.VMEM)
    width, dims = weights.shape
    return pl.pallas_call(
        project_kernel,
        out_shape=jax.ShapeDtypeStruct((n, ROWS, width // n), BF),
        in_specs=[vmem] * (2 + len(terms)),
        out_specs=vmem,
        compiler_params=pltpu.CompilerParams(vmem_limit_bytes=24 * 1024 * 1024),
        cost_estimate=pl.CostEstimate(
            flops=2 * ROWS * width * dims, bytes_accessed=8 << 20, transcendentals=0
        ),
        name="project_kv",
    )(grad, weights, *terms)


def assemble_kernel(where, mine, theirs, out):
    n, _, width = mine.shape
    for k in range(n):
        near = pl.multiple_of((2 * k + where[0]) * width, width)
        far = pl.multiple_of((2 * k + 1 - where[0]) * width, width)
        out[:, pl.ds(near, width)] = mine[k]
        out[:, pl.ds(far, width)] = theirs[k]


def assemble(where, mine, theirs):
    vmem = pl.BlockSpec(memory_space=pltpu.VMEM)
    n, rows, width = mine.shape
    return pl.pallas_call(
        assemble_kernel,
        out_shape=jax.ShapeDtypeStruct((rows, 2 * n * width), BF),
        in_specs=[pl.BlockSpec(memory_space=pltpu.SMEM), vmem, vmem],
        out_specs=vmem,
        compiler_params=pltpu.CompilerParams(vmem_limit_bytes=16 * 1024 * 1024),
        name="assemble",
    )(where, mine, theirs)


def body(queries, key_rows, saved_value_rows, out_grad, doc_lens, w_query, key_weight, value_weight):
    servers = lax.axis_size("server")
    dps = lax.axis_size("dp")
    server = lax.axis_index("server")
    core = lax.axis_index("section")
    odd = server % 2
    both = ("server", "section")

    def swap_pairs(j):
        pairs = []
        for s in range(servers):
            z, a, b = s // 4, (s % 4) // 2, s % 2
            for c in range(2):
                target = z * 4 + 2 * c + (b ^ j)
                pairs.append((2 * s + c, 2 * target + a))
        return pairs

    pairs = [swap_pairs(0), swap_pairs(1)]

    def swap(x, j):
        return lax.ppermute(x, both, pairs[j])

    def shift(x, axis, k):
        n = lax.axis_size(axis)
        return lax.ppermute(x, axis, [(i, (i + k) % n) for i in range(n)])

    def flip(x):
        return lax.ppermute(x, "section", [(0, 1), (1, 0)])

    def groups(left, right):
        half = left.shape[-1] // 2
        first = jnp.concatenate([left[:, :half], right[:, :half]], 1)
        second = jnp.concatenate([left[:, half:], right[:, half:]], 1)
        return jnp.where(odd == 0, first, second), jnp.where(odd == 0, second, first)

    kv_first, kv_second = groups(key_rows[0], saved_value_rows[0])
    block = jnp.concatenate([swap(kv_first, 0), swap(kv_second, 1)], 0)
    blocks = [block]

    queries, out_grad, _ = lax.optimization_barrier((queries, out_grad, block))
    qg_first, qg_second = groups(queries[0], out_grad[0])
    qg0, qg1 = swap(qg_first, 0), swap(qg_second, 1)

    kw_first, kw_second = groups(key_weight, value_weight)
    half = w_query.shape[1] // 2
    weight = jnp.concatenate(
        [kw_first, kw_second, jnp.where(odd == 0, w_query[:, :half], w_query[:, half:])], 1
    )
    half = weight.shape[0] // 2
    mine = jnp.where(core == 0, weight[:half], weight[half:])
    theirs = flip(jnp.where(core == 0, weight[half:], weight[:half]))
    half = 2 * kw_first.shape[1]
    wide = jnp.concatenate(
        [
            mine[:, :half],
            theirs[:, :half],
            jnp.where(core == (server % 4) // 2, mine[:, half:], theirs[:, half:]),
        ],
        1,
    )
    query_weight, kv_weight = [
        lax.all_gather(w, "dp", axis=0, tiled=True)
        for w in (wide[:, 2 * half :], wide[:, : 2 * half])
    ]

    for k in range(1, BACK + 1):
        if k == BACK:
            blocks[-1], qg0, qg1 = lax.optimization_barrier((blocks[-1], qg0, qg1))
        blocks.append(shift(blocks[-1], "server", 4))
    low = jnp.stack(blocks[:BACK])
    high = jnp.stack(blocks[1:])
    other = flip(jnp.where(core == 0, low, high))

    info = jnp.concatenate(
        [
            jnp.stack([(server // 4) * (4 * ROWS), core, odd, server % 4]).astype(jnp.int32),
            jnp.zeros((4,), jnp.int32),
            doc_lens[0].astype(jnp.int32),
        ]
    )
    dq, own_part, other_part = attention(
        info, qg0, qg1, blocks, other, []
    )

    *sent_products, totals, held = project_query(
        info, own_part, flip(other_part), dq, flip(dq), query_weight
    )
    products = [sent_products[0]]
    for k in range(1, 4):
        pairs_x = [(s, s // 4 * 4 + (s + k) % 4) for s in range(servers)]
        products.append(lax.ppermute(sent_products[k], "server", pairs_x))

    for k in range(BACK - 1, -1, -1):
        if k == 1:
            held, products[1], products[3] = lax.optimization_barrier(
                (held, products[1], products[3])
            )
        held = (totals[k] + shift(held, "server", -4).astype(F32)).astype(BF)
    held, products[2] = lax.optimization_barrier((held, products[2]))
    kv_grad = jnp.concatenate([swap(held[:ROWS], 0), swap(held[ROWS:], 1)], 1)
    kv_grad = jnp.concatenate([kv_grad, flip(kv_grad)], 1)
    mine = project(kv_grad, kv_weight, products, dps)
    theirs = flip(mine)
    where = core.astype(jnp.int32)[None]
    return assemble(where, mine, theirs)[None]


def solution(mesh):
    return jax.shard_map(
        body,
        mesh=mesh,
        in_specs=(
            P("dp", "server", "section"),
            P("dp", "server", "section"),
            P("dp", "server", "section"),
            P("dp", "server", "section"),
            P("dp", None),
            P("dp", "section"),
            P("dp", "section"),
            P("dp", "section"),
        ),
        out_specs=P("dp", "server", None),
        check_vma=False,
    )
```

```python
import functools

import jax
import jax.numpy as jnp
from jax import lax
from jax.experimental import pallas as pl
from jax.experimental.pallas import tpu as pltpu
from jax.sharding import PartitionSpec as P

HEAD = 128
GROUP = 4
ROWS = 128
CHUNK = 2 * ROWS
BACK = 4
CHUNKS = 2 * BACK + 1
FACTOR = HEAD**-0.5
FILL = -1e30
LOG2E = 1.4426950408889634
BF = jnp.bfloat16
F32 = jnp.float32


def nt(a, b):
    return lax.dot_general(a, b, (((1,), (1,)), ((), ())), preferred_element_type=F32)


def nn(a, b):
    return lax.dot_general(a, b, (((1,), (0,)), ((), ())), preferred_element_type=F32)


def tn(a, b):
    return lax.dot_general(a, b, (((0,), (0,)), ((), ())), preferred_element_type=F32)


def attention_kernel(info, qg0, qg1, *refs):
    own_in = refs[: BACK + 1]
    other_in = refs[BACK + 1]
    dq, own_out, other_out, kv, s_buf, p_buf, part, q_all, g_all = refs[-9:]
    block_base, core, odd = info[0], info[1], info[2]
    for n in range(BACK + 1):
        kv[n] = own_in[n][...]
    for n in range(BACK):
        kv[BACK + 1 + n] = other_in[n]
    for h in range(GROUP):
        for slot, ref in enumerate((qg0, qg1)):
            q_all[h, slot * ROWS : (slot + 1) * ROWS, :] = ref[:, h * HEAD : (h + 1) * HEAD]
            g_all[h, slot * ROWS : (slot + 1) * ROWS, :] = ref[
                :, (GROUP + h) * HEAD : (GROUP + h + 1) * HEAD
            ]

    lane = lax.broadcasted_iota(jnp.int32, (1, CHUNK), 1)
    query_pos = block_base + core * CHUNK + jnp.bitwise_xor(lane, odd * ROWS)
    doc_first = jnp.zeros_like(query_pos)
    end = info[8]
    for d in range(7):
        if d:
            end = end + info[8 + d]
        doc_first = jnp.where(query_pos >= end, end, doc_first)
    key_row = jnp.bitwise_xor(
        lax.broadcasted_iota(jnp.int32, (CHUNK, CHUNK), 0), odd * ROWS
    )

    def chunk_base(n):
        own = block_base - n * 2 * CHUNK + core * CHUNK
        i = n - (BACK + 1)
        other = jnp.where(core == 0, block_base - (i + 1) * 2 * CHUNK + CHUNK, block_base - i * 2 * CHUNK)
        return jnp.where(n <= BACK, own, other)

    def score_step(n, peak):
        base = chunk_base(n)
        visible = (key_row >= doc_first - base) & (key_row <= query_pos - base)
        keys = kv[n, :, :HEAD]
        out = []
        for h in range(GROUP):
            s = jnp.where(visible, nt(keys, q_all[h]), FILL)
            s_buf[n, h] = s
            out.append(jnp.maximum(peak[h], jnp.max(s.reshape(CHUNK // 8, 8, CHUNK), axis=0)))
        return tuple(out)

    peak = lax.fori_loop(
        0, CHUNKS, score_step, tuple(jnp.full((8, CHUNK), FILL, F32) for _ in range(GROUP))
    )
    peak = [jnp.max(m, axis=0, keepdims=True) for m in peak]

    def weight_step(n, carry):
        totals, deltas = carry
        values = kv[n, :, HEAD:]
        new_t, new_d = [], []
        for h in range(GROUP):
            e = jnp.exp2((s_buf[n, h] - peak[h]) * (FACTOR * LOG2E))
            dp = nt(values, g_all[h])
            s_buf[n, h] = e
            p_buf[n, h] = dp
            new_t.append(totals[h] + jnp.sum(e.reshape(CHUNK // 8, 8, CHUNK), axis=0))
            new_d.append(deltas[h] + jnp.sum((e * dp).reshape(CHUNK // 8, 8, CHUNK), axis=0))
        return tuple(new_t), tuple(new_d)

    zero = tuple(jnp.zeros((8, CHUNK), F32) for _ in range(GROUP))
    totals, deltas = lax.fori_loop(0, CHUNKS, weight_step, (zero, zero))
    inverse = [1.0 / jnp.sum(t, axis=0, keepdims=True) for t in totals]
    delta = [jnp.sum(d, axis=0, keepdims=True) * inverse[h] for h, d in enumerate(deltas)]

    def grad_step(n, acc):
        keys = kv[n, :, :HEAD]
        dk = jnp.zeros((CHUNK, HEAD), F32)
        dv = jnp.zeros((CHUNK, HEAD), F32)
        out = []
        for h in range(GROUP):
            w = s_buf[n, h] * inverse[h]
            ds = (w * (p_buf[n, h] - delta[h])).astype(BF)
            w = w.astype(BF)
            dv = dv + nn(w, g_all[h])
            dk = dk + nn(ds, q_all[h])
            out.append(acc[h] + tn(keys, ds))
        part[n, :, :HEAD] = dk * FACTOR
        part[n, :, HEAD:] = dv
        return tuple(out)

    acc = lax.fori_loop(
        0, CHUNKS, grad_step, tuple(jnp.zeros((HEAD, CHUNK), F32) for _ in range(GROUP))
    )
    for h in range(GROUP):
        dq[:, h * HEAD : (h + 1) * HEAD] = (jnp.transpose(acc[h]) * FACTOR).astype(BF)
    for n in range(BACK + 1):
        own_out[n] = part[n]
    for n in range(BACK):
        other_out[n] = part[BACK + 1 + n].astype(BF)


def attention(info, qg0, qg1, own_blocks, other_blocks, after):
    vmem = pl.BlockSpec(memory_space=pltpu.VMEM)
    return pl.pallas_call(
        attention_kernel,
        out_shape=(
            jax.ShapeDtypeStruct((CHUNK, GROUP * HEAD), BF),
            jax.ShapeDtypeStruct((BACK + 1, CHUNK, 2 * HEAD), F32),
            jax.ShapeDtypeStruct((BACK, CHUNK, 2 * HEAD), BF),
        ),
        in_specs=[pl.BlockSpec(memory_space=pltpu.SMEM)]
        + [vmem] * (BACK + 4)
        + [pl.BlockSpec(memory_space=pl.ANY)] * len(after),
        out_specs=(vmem,) * 3,
        scratch_shapes=[
            pltpu.VMEM((CHUNKS, CHUNK, 2 * HEAD), BF),
            pltpu.VMEM((CHUNKS, GROUP, CHUNK, CHUNK), F32),
            pltpu.VMEM((CHUNKS, GROUP, CHUNK, CHUNK), F32),
            pltpu.VMEM((CHUNKS, CHUNK, 2 * HEAD), F32),
            pltpu.VMEM((GROUP, CHUNK, HEAD), BF),
            pltpu.VMEM((GROUP, CHUNK, HEAD), BF),
        ],
        compiler_params=pltpu.CompilerParams(vmem_limit_bytes=30 * 1024 * 1024),
        cost_estimate=pl.CostEstimate(
            flops=5 * 2 * CHUNKS * GROUP * CHUNK * CHUNK * HEAD,
            bytes_accessed=8 << 20,
            transcendentals=CHUNKS * GROUP * CHUNK * CHUNK,
        ),
        name="attention_grads",
    )(info, qg0, qg1, *own_blocks, other_blocks, *after)


def project_query_kernel(info, own, arrived, dq, other, *refs):
    weights, *outs, totals, held, rows = refs
    core, odd, chip = info[1], info[2], info[3]
    for k in range(BACK + 1):
        near = arrived[k].astype(F32) if k < BACK else 0.0
        far = arrived[k - 1].astype(F32) if k else 0.0
        total = own[k] + jnp.where(core == 0, near, far)
        if k < BACK:
            totals[k] = total
        else:
            held[...] = total.astype(BF)
    for source, c in ((dq, core), (other, 1 - core)):
        for slot in range(2):
            owner = 2 * c + jnp.bitwise_xor(odd, slot)
            at = pl.multiple_of(lax.rem(owner - chip + 4, 4) * ROWS, ROWS)
            rows[pl.ds(at, ROWS), :] = source[slot * ROWS : (slot + 1) * ROWS, :]
    width = 4 * ROWS
    for k in range(weights.shape[0] // width):
        product = nt(rows[...], weights[k * width : (k + 1) * width]).astype(BF)
        for i in range(4):
            outs[i][:, k * width : (k + 1) * width] = product[i * ROWS : (i + 1) * ROWS]


def project_query(info, own, arrived, dq, other, weights):
    vmem = pl.BlockSpec(memory_space=pltpu.VMEM)
    width, dims = weights.shape
    return pl.pallas_call(
        project_query_kernel,
        out_shape=(jax.ShapeDtypeStruct((ROWS, width), BF),) * 4
        + (
            jax.ShapeDtypeStruct((BACK,) + own.shape[1:], F32),
            jax.ShapeDtypeStruct(own.shape[1:], BF),
        ),
        in_specs=[pl.BlockSpec(memory_space=pltpu.SMEM)]
        + [vmem] * 5,
        out_specs=(vmem,) * 6,
        scratch_shapes=[pltpu.VMEM((4 * ROWS, dims), BF)],
        compiler_params=pltpu.CompilerParams(vmem_limit_bytes=24 * 1024 * 1024),
        cost_estimate=pl.CostEstimate(
            flops=8 * ROWS * width * dims, bytes_accessed=4 << 20, transcendentals=0
        ),
        name="project_query",
    )(info, own, arrived, dq, other, weights)


def project_kernel(grad, weights, *refs):
    *terms, out = refs
    n, _, width = out.shape
    for k in range(n):
        at = slice(k * width, (k + 1) * width)
        total = nt(grad[...], weights[at])
        for term in terms:
            total = total + term[:, at].astype(F32)
        out[k] = total.astype(BF)


def project(grad, weights, terms, n):
    vmem = pl.BlockSpec(memory_space=pltpu.VMEM)
    width, dims = weights.shape
    return pl.pallas_call(
        project_kernel,
        out_shape=jax.ShapeDtypeStruct((n, ROWS, width // n), BF),
        in_specs=[vmem] * (2 + len(terms)),
        out_specs=vmem,
        compiler_params=pltpu.CompilerParams(vmem_limit_bytes=24 * 1024 * 1024),
        cost_estimate=pl.CostEstimate(
            flops=2 * ROWS * width * dims, bytes_accessed=8 << 20, transcendentals=0
        ),
        name="project_kv",
    )(grad, weights, *terms)


def assemble_kernel(where, mine, theirs, out):
    n, _, width = mine.shape
    for k in range(n):
        near = pl.multiple_of((2 * k + where[0]) * width, width)
        far = pl.multiple_of((2 * k + 1 - where[0]) * width, width)
        out[:, pl.ds(near, width)] = mine[k]
        out[:, pl.ds(far, width)] = theirs[k]


def assemble(where, mine, theirs):
    vmem = pl.BlockSpec(memory_space=pltpu.VMEM)
    n, rows, width = mine.shape
    return pl.pallas_call(
        assemble_kernel,
        out_shape=jax.ShapeDtypeStruct((rows, 2 * n * width), BF),
        in_specs=[pl.BlockSpec(memory_space=pltpu.SMEM), vmem, vmem],
        out_specs=vmem,
        compiler_params=pltpu.CompilerParams(vmem_limit_bytes=16 * 1024 * 1024),
        name="assemble",
    )(where, mine, theirs)


def body(queries, key_rows, saved_value_rows, out_grad, doc_lens, w_query, key_weight, value_weight):
    servers = lax.axis_size("server")
    dps = lax.axis_size("dp")
    server = lax.axis_index("server")
    core = lax.axis_index("section")
    odd = server % 2
    both = ("server", "section")

    def swap_pairs(j):
        pairs = []
        for s in range(servers):
            z, a, b = s // 4, (s % 4) // 2, s % 2
            for c in range(2):
                target = z * 4 + 2 * c + (b ^ j)
                pairs.append((2 * s + c, 2 * target + a))
        return pairs

    pairs = [swap_pairs(0), swap_pairs(1)]

    def swap(x, j):
        return lax.ppermute(x, both, pairs[j])

    def shift(x, axis, k):
        n = lax.axis_size(axis)
        return lax.ppermute(x, axis, [(i, (i + k) % n) for i in range(n)])

    def flip(x):
        return lax.ppermute(x, "section", [(0, 1), (1, 0)])

    def groups(left, right):
        half = left.shape[-1] // 2
        first = jnp.concatenate([left[:, :half], right[:, :half]], 1)
        second = jnp.concatenate([left[:, half:], right[:, half:]], 1)
        return jnp.where(odd == 0, first, second), jnp.where(odd == 0, second, first)

    kv_first, kv_second = groups(key_rows[0], saved_value_rows[0])
    block = jnp.concatenate([swap(kv_first, 0), swap(kv_second, 1)], 0)
    blocks = [block]

    queries, out_grad, _ = lax.optimization_barrier((queries, out_grad, block))
    qg_first, qg_second = groups(queries[0], out_grad[0])
    qg0, qg1 = swap(qg_first, 0), swap(qg_second, 1)

    kw_first, kw_second = groups(key_weight, value_weight)
    half = w_query.shape[1] // 2
    weight = jnp.concatenate(
        [kw_first, kw_second, jnp.where(odd == 0, w_query[:, :half], w_query[:, half:])], 1
    )
    half = weight.shape[0] // 2
    mine = jnp.where(core == 0, weight[:half], weight[half:])
    theirs = flip(jnp.where(core == 0, weight[half:], weight[:half]))
    half = 2 * kw_first.shape[1]
    after, _ = lax.optimization_barrier((core, block))
    query_weight = jnp.where(after == (server % 4) // 2, mine[:, half:], theirs[:, half:])
    query_weight = lax.all_gather(query_weight, "dp", axis=0, tiled=True)
    for k in range(1, BACK + 1):
        if k == BACK:
            blocks[-1], qg0, qg1 = lax.optimization_barrier((blocks[-1], qg0, qg1))
        blocks.append(shift(blocks[-1], "server", 4))
    after, _ = lax.optimization_barrier((core, blocks[1]))
    kv_weight = jnp.concatenate(
        [mine[:, :half], jnp.where(after >= 0, theirs[:, :half], mine[:, :half])], 1
    )
    kv_weight = lax.all_gather(kv_weight, "dp", axis=0, tiled=True)

    low = jnp.stack(blocks[:BACK])
    high = jnp.stack(blocks[1:])
    other = flip(jnp.where(core == 0, low, high))

    info = jnp.concatenate(
        [
            jnp.stack([(server // 4) * (4 * ROWS), core, odd, server % 4]).astype(jnp.int32),
            jnp.zeros((4,), jnp.int32),
            doc_lens[0].astype(jnp.int32),
        ]
    )
    dq, own_part, other_part = attention(
        info, qg0, qg1, blocks, other, []
    )

    *sent_products, totals, held = project_query(
        info, own_part, flip(other_part), dq, flip(dq), query_weight
    )
    products = [sent_products[0]]
    for k in range(1, 4):
        pairs_x = [(s, s // 4 * 4 + (s + k) % 4) for s in range(servers)]
        products.append(lax.ppermute(sent_products[k], "server", pairs_x))

    for k in range(BACK - 1, -1, -1):
        if k == 1:
            held, products[1], products[3] = lax.optimization_barrier(
                (held, products[1], products[3])
            )
        held = (totals[k] + shift(held, "server", -4).astype(F32)).astype(BF)
    held, products[2] = lax.optimization_barrier((held, products[2]))
    kv_grad = jnp.concatenate([swap(held[:ROWS], 0), swap(held[ROWS:], 1)], 1)
    kv_grad = jnp.concatenate([kv_grad, flip(kv_grad)], 1)
    mine = project(kv_grad, kv_weight, products, dps)
    theirs = flip(mine)
    where = core.astype(jnp.int32)[None]
    return assemble(where, mine, theirs)[None]


def solution(mesh):
    return jax.shard_map(
        body,
        mesh=mesh,
        in_specs=(
            P("dp", "server", "section"),
            P("dp", "server", "section"),
            P("dp", "server", "section"),
            P("dp", "server", "section"),
            P("dp", None),
            P("dp", "section"),
            P("dp", "section"),
            P("dp", "section"),
        ),
        out_specs=P("dp", "server", None),
        check_vma=False,
    )
```

```python
import functools

import jax
import jax.numpy as jnp
from jax import lax
from jax.experimental import pallas as pl
from jax.experimental.pallas import tpu as pltpu
from jax.sharding import PartitionSpec as P

HEAD = 128
GROUP = 4
ROWS = 128
CHUNK = 2 * ROWS
BACK = 4
CHUNKS = 2 * BACK + 1
FACTOR = HEAD**-0.5
FILL = -1e30
LOG2E = 1.4426950408889634
BF = jnp.bfloat16
F32 = jnp.float32


def nt(a, b):
    return lax.dot_general(a, b, (((1,), (1,)), ((), ())), preferred_element_type=F32)


def nn(a, b):
    return lax.dot_general(a, b, (((1,), (0,)), ((), ())), preferred_element_type=F32)


def tn(a, b):
    return lax.dot_general(a, b, (((0,), (0,)), ((), ())), preferred_element_type=F32)


def attention_kernel(info, qg0, qg1, *refs):
    own_in = refs[: BACK + 1]
    other_in = refs[BACK + 1]
    dq, own_out, other_out, kv, s_buf, p_buf, part, q_all, g_all = refs[-9:]
    block_base, core, odd = info[0], info[1], info[2]
    for n in range(BACK + 1):
        kv[n] = own_in[n][...]
    for n in range(BACK):
        kv[BACK + 1 + n] = other_in[n]
    for h in range(GROUP):
        for slot, ref in enumerate((qg0, qg1)):
            q_all[h, slot * ROWS : (slot + 1) * ROWS, :] = ref[:, h * HEAD : (h + 1) * HEAD]
            g_all[h, slot * ROWS : (slot + 1) * ROWS, :] = ref[
                :, (GROUP + h) * HEAD : (GROUP + h + 1) * HEAD
            ]

    lane = lax.broadcasted_iota(jnp.int32, (1, CHUNK), 1)
    query_pos = block_base + core * CHUNK + jnp.bitwise_xor(lane, odd * ROWS)
    doc_first = jnp.zeros_like(query_pos)
    end = info[8]
    for d in range(7):
        if d:
            end = end + info[8 + d]
        doc_first = jnp.where(query_pos >= end, end, doc_first)
    key_row = jnp.bitwise_xor(
        lax.broadcasted_iota(jnp.int32, (CHUNK, CHUNK), 0), odd * ROWS
    )

    def chunk_base(n):
        own = block_base - n * 2 * CHUNK + core * CHUNK
        i = n - (BACK + 1)
        other = jnp.where(core == 0, block_base - (i + 1) * 2 * CHUNK + CHUNK, block_base - i * 2 * CHUNK)
        return jnp.where(n <= BACK, own, other)

    def score_step(n, peak):
        base = chunk_base(n)
        visible = (key_row >= doc_first - base) & (key_row <= query_pos - base)
        keys = kv[n, :, :HEAD]
        out = []
        for h in range(GROUP):
            s = jnp.where(visible, nt(keys, q_all[h]), FILL)
            s_buf[n, h] = s
            out.append(jnp.maximum(peak[h], jnp.max(s.reshape(CHUNK // 8, 8, CHUNK), axis=0)))
        return tuple(out)

    peak = lax.fori_loop(
        0, CHUNKS, score_step, tuple(jnp.full((8, CHUNK), FILL, F32) for _ in range(GROUP))
    )
    peak = [jnp.max(m, axis=0, keepdims=True) for m in peak]

    def weight_step(n, carry):
        totals, deltas = carry
        values = kv[n, :, HEAD:]
        new_t, new_d = [], []
        for h in range(GROUP):
            e = jnp.exp2((s_buf[n, h] - peak[h]) * (FACTOR * LOG2E))
            dp = nt(values, g_all[h])
            s_buf[n, h] = e
            p_buf[n, h] = dp
            new_t.append(totals[h] + jnp.sum(e.reshape(CHUNK // 8, 8, CHUNK), axis=0))
            new_d.append(deltas[h] + jnp.sum((e * dp).reshape(CHUNK // 8, 8, CHUNK), axis=0))
        return tuple(new_t), tuple(new_d)

    zero = tuple(jnp.zeros((8, CHUNK), F32) for _ in range(GROUP))
    totals, deltas = lax.fori_loop(0, CHUNKS, weight_step, (zero, zero))
    inverse = [1.0 / jnp.sum(t, axis=0, keepdims=True) for t in totals]
    delta = [jnp.sum(d, axis=0, keepdims=True) * inverse[h] for h, d in enumerate(deltas)]

    def grad_step(n, acc):
        keys = kv[n, :, :HEAD]
        dk = jnp.zeros((CHUNK, HEAD), F32)
        dv = jnp.zeros((CHUNK, HEAD), F32)
        out = []
        for h in range(GROUP):
            w = s_buf[n, h] * inverse[h]
            ds = (w * (p_buf[n, h] - delta[h])).astype(BF)
            w = w.astype(BF)
            dv = dv + nn(w, g_all[h])
            dk = dk + nn(ds, q_all[h])
            out.append(acc[h] + tn(keys, ds))
        part[n, :, :HEAD] = dk * FACTOR
        part[n, :, HEAD:] = dv
        return tuple(out)

    acc = lax.fori_loop(
        0, CHUNKS, grad_step, tuple(jnp.zeros((HEAD, CHUNK), F32) for _ in range(GROUP))
    )
    for h in range(GROUP):
        dq[:, h * HEAD : (h + 1) * HEAD] = (jnp.transpose(acc[h]) * FACTOR).astype(BF)
    for n in range(BACK + 1):
        own_out[n] = part[n]
    for n in range(BACK):
        other_out[n] = part[BACK + 1 + n].astype(BF)


def attention(info, qg0, qg1, own_blocks, other_blocks, after):
    vmem = pl.BlockSpec(memory_space=pltpu.VMEM)
    return pl.pallas_call(
        attention_kernel,
        out_shape=(
            jax.ShapeDtypeStruct((CHUNK, GROUP * HEAD), BF),
            jax.ShapeDtypeStruct((BACK + 1, CHUNK, 2 * HEAD), F32),
            jax.ShapeDtypeStruct((BACK, CHUNK, 2 * HEAD), BF),
        ),
        in_specs=[pl.BlockSpec(memory_space=pltpu.SMEM)]
        + [vmem] * (BACK + 4)
        + [pl.BlockSpec(memory_space=pl.ANY)] * len(after),
        out_specs=(vmem,) * 3,
        scratch_shapes=[
            pltpu.VMEM((CHUNKS, CHUNK, 2 * HEAD), BF),
            pltpu.VMEM((CHUNKS, GROUP, CHUNK, CHUNK), F32),
            pltpu.VMEM((CHUNKS, GROUP, CHUNK, CHUNK), F32),
            pltpu.VMEM((CHUNKS, CHUNK, 2 * HEAD), F32),
            pltpu.VMEM((GROUP, CHUNK, HEAD), BF),
            pltpu.VMEM((GROUP, CHUNK, HEAD), BF),
        ],
        compiler_params=pltpu.CompilerParams(vmem_limit_bytes=30 * 1024 * 1024),
        cost_estimate=pl.CostEstimate(
            flops=5 * 2 * CHUNKS * GROUP * CHUNK * CHUNK * HEAD,
            bytes_accessed=8 << 20,
            transcendentals=CHUNKS * GROUP * CHUNK * CHUNK,
        ),
        name="attention_grads",
    )(info, qg0, qg1, *own_blocks, other_blocks, *after)


def project_query_kernel(info, own, arrived, dq, other, *refs):
    weights, *outs, totals, held, rows = refs
    core, odd, chip = info[1], info[2], info[3]
    for k in range(BACK + 1):
        near = arrived[k].astype(F32) if k < BACK else 0.0
        far = arrived[k - 1].astype(F32) if k else 0.0
        total = own[k] + jnp.where(core == 0, near, far)
        if k < BACK:
            totals[k] = total
        else:
            held[...] = total.astype(BF)
    for source, c in ((dq, core), (other, 1 - core)):
        for slot in range(2):
            owner = 2 * c + jnp.bitwise_xor(odd, slot)
            at = pl.multiple_of(lax.rem(owner - chip + 4, 4) * ROWS, ROWS)
            rows[pl.ds(at, ROWS), :] = source[slot * ROWS : (slot + 1) * ROWS, :]
    width = 4 * ROWS
    for k in range(weights.shape[0] // width):
        product = nt(rows[...], weights[k * width : (k + 1) * width]).astype(BF)
        for i in range(4):
            outs[i][:, k * width : (k + 1) * width] = product[i * ROWS : (i + 1) * ROWS]


def project_query(info, own, arrived, dq, other, weights):
    vmem = pl.BlockSpec(memory_space=pltpu.VMEM)
    width, dims = weights.shape
    return pl.pallas_call(
        project_query_kernel,
        out_shape=(jax.ShapeDtypeStruct((ROWS, width), BF),) * 4
        + (
            jax.ShapeDtypeStruct((BACK,) + own.shape[1:], F32),
            jax.ShapeDtypeStruct(own.shape[1:], BF),
        ),
        in_specs=[pl.BlockSpec(memory_space=pltpu.SMEM)]
        + [vmem] * 5,
        out_specs=(vmem,) * 6,
        scratch_shapes=[pltpu.VMEM((4 * ROWS, dims), BF)],
        compiler_params=pltpu.CompilerParams(vmem_limit_bytes=24 * 1024 * 1024),
        cost_estimate=pl.CostEstimate(
            flops=8 * ROWS * width * dims, bytes_accessed=4 << 20, transcendentals=0
        ),
        name="project_query",
    )(info, own, arrived, dq, other, weights)


def project_kernel(grad, weights, *refs):
    *terms, out = refs
    n, _, width = out.shape
    for k in range(n):
        at = slice(k * width, (k + 1) * width)
        total = nt(grad[...], weights[at])
        for term in terms:
            total = total + term[:, at].astype(F32)
        out[k] = total.astype(BF)


def project(grad, weights, terms, n):
    vmem = pl.BlockSpec(memory_space=pltpu.VMEM)
    width, dims = weights.shape
    return pl.pallas_call(
        project_kernel,
        out_shape=jax.ShapeDtypeStruct((n, ROWS, width // n), BF),
        in_specs=[vmem] * (2 + len(terms)),
        out_specs=vmem,
        compiler_params=pltpu.CompilerParams(vmem_limit_bytes=24 * 1024 * 1024),
        cost_estimate=pl.CostEstimate(
            flops=2 * ROWS * width * dims, bytes_accessed=8 << 20, transcendentals=0
        ),
        name="project_kv",
    )(grad, weights, *terms)


def assemble_kernel(where, mine, theirs, out):
    n, _, width = mine.shape
    for k in range(n):
        near = pl.multiple_of((2 * k + where[0]) * width, width)
        far = pl.multiple_of((2 * k + 1 - where[0]) * width, width)
        out[:, pl.ds(near, width)] = mine[k]
        out[:, pl.ds(far, width)] = theirs[k]


def assemble(where, mine, theirs):
    vmem = pl.BlockSpec(memory_space=pltpu.VMEM)
    n, rows, width = mine.shape
    return pl.pallas_call(
        assemble_kernel,
        out_shape=jax.ShapeDtypeStruct((rows, 2 * n * width), BF),
        in_specs=[pl.BlockSpec(memory_space=pltpu.SMEM), vmem, vmem],
        out_specs=vmem,
        compiler_params=pltpu.CompilerParams(vmem_limit_bytes=16 * 1024 * 1024),
        name="assemble",
    )(where, mine, theirs)


def body(queries, key_rows, saved_value_rows, out_grad, doc_lens, w_query, key_weight, value_weight):
    servers = lax.axis_size("server")
    dps = lax.axis_size("dp")
    server = lax.axis_index("server")
    core = lax.axis_index("section")
    odd = server % 2
    both = ("server", "section")

    def swap_pairs(j):
        pairs = []
        for s in range(servers):
            z, a, b = s // 4, (s % 4) // 2, s % 2
            for c in range(2):
                target = z * 4 + 2 * c + (b ^ j)
                pairs.append((2 * s + c, 2 * target + a))
        return pairs

    pairs = [swap_pairs(0), swap_pairs(1)]

    def swap(x, j):
        return lax.ppermute(x, both, pairs[j])

    def shift(x, axis, k):
        n = lax.axis_size(axis)
        return lax.ppermute(x, axis, [(i, (i + k) % n) for i in range(n)])

    def flip(x):
        return lax.ppermute(x, "section", [(0, 1), (1, 0)])

    def groups(left, right):
        half = left.shape[-1] // 2
        first = jnp.concatenate([left[:, :half], right[:, :half]], 1)
        second = jnp.concatenate([left[:, half:], right[:, half:]], 1)
        return jnp.where(odd == 0, first, second), jnp.where(odd == 0, second, first)

    kv_first, kv_second = groups(key_rows[0], saved_value_rows[0])
    block = jnp.concatenate([swap(kv_first, 0), swap(kv_second, 1)], 0)
    blocks = [block]

    queries, out_grad, _ = lax.optimization_barrier((queries, out_grad, block))
    qg_first, qg_second = groups(queries[0], out_grad[0])
    qg0, qg1 = swap(qg_first, 0), swap(qg_second, 1)

    kw_first, kw_second = groups(key_weight, value_weight)
    half = w_query.shape[1] // 2
    weight = jnp.concatenate(
        [kw_first, kw_second, jnp.where(odd == 0, w_query[:, :half], w_query[:, half:])], 1
    )
    half = weight.shape[0] // 2
    mine = jnp.where(core == 0, weight[:half], weight[half:])
    theirs = flip(jnp.where(core == 0, weight[half:], weight[:half]))
    half = 2 * kw_first.shape[1]
    after, _ = lax.optimization_barrier((core, block))
    query_weight = jnp.where(after == (server % 4) // 2, mine[:, half:], theirs[:, half:])
    query_weight = lax.all_gather(query_weight, "dp", axis=0, tiled=True)
    kv_weight = jnp.concatenate(
        [mine[:, :half], jnp.where(after >= 0, theirs[:, :half], mine[:, :half])], 1
    )
    kv_weight = lax.all_gather(kv_weight, "dp", axis=0, tiled=True)

    for k in range(1, BACK + 1):
        if k == BACK:
            blocks[-1], qg0, qg1 = lax.optimization_barrier((blocks[-1], qg0, qg1))
        blocks.append(shift(blocks[-1], "server", 4))
    low = jnp.stack(blocks[:BACK])
    high = jnp.stack(blocks[1:])
    other = flip(jnp.where(core == 0, low, high))

    info = jnp.concatenate(
        [
            jnp.stack([(server // 4) * (4 * ROWS), core, odd, server % 4]).astype(jnp.int32),
            jnp.zeros((4,), jnp.int32),
            doc_lens[0].astype(jnp.int32),
        ]
    )
    dq, own_part, other_part = attention(
        info, qg0, qg1, blocks, other, []
    )

    *sent_products, totals, held = project_query(
        info, own_part, flip(other_part), dq, flip(dq), query_weight
    )
    products = [sent_products[0]]
    for k in range(1, 4):
        pairs_x = [(s, s // 4 * 4 + (s + k) % 4) for s in range(servers)]
        products.append(lax.ppermute(sent_products[k], "server", pairs_x))

    for k in range(BACK - 1, -1, -1):
        if k == 1:
            held, products[1], products[3] = lax.optimization_barrier(
                (held, products[1], products[3])
            )
        held = (totals[k] + shift(held, "server", -4).astype(F32)).astype(BF)
    held, products[2] = lax.optimization_barrier((held, products[2]))
    kv_grad = jnp.concatenate([swap(held[:ROWS], 0), swap(held[ROWS:], 1)], 1)
    kv_grad = jnp.concatenate([kv_grad, flip(kv_grad)], 1)
    mine = project(kv_grad, kv_weight, products, dps)
    theirs = flip(mine)
    where = core.astype(jnp.int32)[None]
    return assemble(where, mine, theirs)[None]


def solution(mesh):
    return jax.shard_map(
        body,
        mesh=mesh,
        in_specs=(
            P("dp", "server", "section"),
            P("dp", "server", "section"),
            P("dp", "server", "section"),
            P("dp", "server", "section"),
            P("dp", None),
            P("dp", "section"),
            P("dp", "section"),
            P("dp", "section"),
        ),
        out_specs=P("dp", "server", None),
        check_vma=False,
    )
```

```python
import functools

import jax
import jax.numpy as jnp
from jax import lax
from jax.experimental import pallas as pl
from jax.experimental.pallas import tpu as pltpu
from jax.sharding import PartitionSpec as P

HEAD = 128
GROUP = 4
ROWS = 128
CHUNK = 2 * ROWS
BACK = 4
CHUNKS = 2 * BACK + 1
FACTOR = HEAD**-0.5
FILL = -1e30
LOG2E = 1.4426950408889634
BF = jnp.bfloat16
F32 = jnp.float32


def nt(a, b):
    return lax.dot_general(a, b, (((1,), (1,)), ((), ())), preferred_element_type=F32)


def nn(a, b):
    return lax.dot_general(a, b, (((1,), (0,)), ((), ())), preferred_element_type=F32)


def tn(a, b):
    return lax.dot_general(a, b, (((0,), (0,)), ((), ())), preferred_element_type=F32)


def attention_kernel(info, qg0, qg1, *refs):
    own_in = refs[: BACK + 1]
    other_in = refs[BACK + 1]
    dq, own_out, other_out, kv, s_buf, p_buf, part, q_all, g_all = refs[-9:]
    block_base, core, odd = info[0], info[1], info[2]
    for n in range(BACK + 1):
        kv[n] = own_in[n][...]
    for n in range(BACK):
        kv[BACK + 1 + n] = other_in[n]
    for h in range(GROUP):
        for slot, ref in enumerate((qg0, qg1)):
            q_all[h, slot * ROWS : (slot + 1) * ROWS, :] = ref[:, h * HEAD : (h + 1) * HEAD]
            g_all[h, slot * ROWS : (slot + 1) * ROWS, :] = ref[
                :, (GROUP + h) * HEAD : (GROUP + h + 1) * HEAD
            ]

    lane = lax.broadcasted_iota(jnp.int32, (1, CHUNK), 1)
    query_pos = block_base + core * CHUNK + jnp.bitwise_xor(lane, odd * ROWS)
    doc_first = jnp.zeros_like(query_pos)
    end = info[8]
    for d in range(7):
        if d:
            end = end + info[8 + d]
        doc_first = jnp.where(query_pos >= end, end, doc_first)
    key_row = jnp.bitwise_xor(
        lax.broadcasted_iota(jnp.int32, (CHUNK, CHUNK), 0), odd * ROWS
    )

    def chunk_base(n):
        own = block_base - n * 2 * CHUNK + core * CHUNK
        i = n - (BACK + 1)
        other = jnp.where(core == 0, block_base - (i + 1) * 2 * CHUNK + CHUNK, block_base - i * 2 * CHUNK)
        return jnp.where(n <= BACK, own, other)

    def score_step(n, peak):
        base = chunk_base(n)
        visible = (key_row >= doc_first - base) & (key_row <= query_pos - base)
        keys = kv[n, :, :HEAD]
        out = []
        for h in range(GROUP):
            s = jnp.where(visible, nt(keys, q_all[h]), FILL)
            s_buf[n, h] = s
            out.append(jnp.maximum(peak[h], jnp.max(s.reshape(CHUNK // 8, 8, CHUNK), axis=0)))
        return tuple(out)

    peak = lax.fori_loop(
        0, CHUNKS, score_step, tuple(jnp.full((8, CHUNK), FILL, F32) for _ in range(GROUP))
    )
    peak = [jnp.max(m, axis=0, keepdims=True) for m in peak]

    def weight_step(n, carry):
        totals, deltas = carry
        values = kv[n, :, HEAD:]
        new_t, new_d = [], []
        for h in range(GROUP):
            e = jnp.exp2((s_buf[n, h] - peak[h]) * (FACTOR * LOG2E))
            dp = nt(values, g_all[h])
            s_buf[n, h] = e
            p_buf[n, h] = dp
            new_t.append(totals[h] + jnp.sum(e.reshape(CHUNK // 8, 8, CHUNK), axis=0))
            new_d.append(deltas[h] + jnp.sum((e * dp).reshape(CHUNK // 8, 8, CHUNK), axis=0))
        return tuple(new_t), tuple(new_d)

    zero = tuple(jnp.zeros((8, CHUNK), F32) for _ in range(GROUP))
    totals, deltas = lax.fori_loop(0, CHUNKS, weight_step, (zero, zero))
    inverse = [1.0 / jnp.sum(t, axis=0, keepdims=True) for t in totals]
    delta = [jnp.sum(d, axis=0, keepdims=True) * inverse[h] for h, d in enumerate(deltas)]

    def grad_step(n, acc):
        keys = kv[n, :, :HEAD]
        dk = jnp.zeros((CHUNK, HEAD), F32)
        dv = jnp.zeros((CHUNK, HEAD), F32)
        out = []
        for h in range(GROUP):
            w = s_buf[n, h] * inverse[h]
            ds = (w * (p_buf[n, h] - delta[h])).astype(BF)
            w = w.astype(BF)
            dv = dv + nn(w, g_all[h])
            dk = dk + nn(ds, q_all[h])
            out.append(acc[h] + tn(keys, ds))
        part[n, :, :HEAD] = dk * FACTOR
        part[n, :, HEAD:] = dv
        return tuple(out)

    acc = lax.fori_loop(
        0, CHUNKS, grad_step, tuple(jnp.zeros((HEAD, CHUNK), F32) for _ in range(GROUP))
    )
    for h in range(GROUP):
        dq[:, h * HEAD : (h + 1) * HEAD] = (jnp.transpose(acc[h]) * FACTOR).astype(BF)
    for n in range(BACK + 1):
        own_out[n] = part[n]
    for n in range(BACK):
        other_out[n] = part[BACK + 1 + n].astype(BF)


def attention(info, qg0, qg1, own_blocks, other_blocks, after):
    vmem = pl.BlockSpec(memory_space=pltpu.VMEM)
    return pl.pallas_call(
        attention_kernel,
        out_shape=(
            jax.ShapeDtypeStruct((CHUNK, GROUP * HEAD), BF),
            jax.ShapeDtypeStruct((BACK + 1, CHUNK, 2 * HEAD), F32),
            jax.ShapeDtypeStruct((BACK, CHUNK, 2 * HEAD), BF),
        ),
        in_specs=[pl.BlockSpec(memory_space=pltpu.SMEM)]
        + [vmem] * (BACK + 4)
        + [pl.BlockSpec(memory_space=pl.ANY)] * len(after),
        out_specs=(vmem,) * 3,
        scratch_shapes=[
            pltpu.VMEM((CHUNKS, CHUNK, 2 * HEAD), BF),
            pltpu.VMEM((CHUNKS, GROUP, CHUNK, CHUNK), F32),
            pltpu.VMEM((CHUNKS, GROUP, CHUNK, CHUNK), F32),
            pltpu.VMEM((CHUNKS, CHUNK, 2 * HEAD), F32),
            pltpu.VMEM((GROUP, CHUNK, HEAD), BF),
            pltpu.VMEM((GROUP, CHUNK, HEAD), BF),
        ],
        compiler_params=pltpu.CompilerParams(vmem_limit_bytes=30 * 1024 * 1024),
        cost_estimate=pl.CostEstimate(
            flops=5 * 2 * CHUNKS * GROUP * CHUNK * CHUNK * HEAD,
            bytes_accessed=8 << 20,
            transcendentals=CHUNKS * GROUP * CHUNK * CHUNK,
        ),
        name="attention_grads",
    )(info, qg0, qg1, *own_blocks, other_blocks, *after)


def project_query_kernel(info, own, arrived, dq, other, *refs):
    weights, *outs, totals, held, rows = refs
    core, odd, chip = info[1], info[2], info[3]
    for k in range(BACK + 1):
        near = arrived[k].astype(F32) if k < BACK else 0.0
        far = arrived[k - 1].astype(F32) if k else 0.0
        total = own[k] + jnp.where(core == 0, near, far)
        if k < BACK:
            totals[k] = total
        else:
            held[...] = total.astype(BF)
    for source, c in ((dq, core), (other, 1 - core)):
        for slot in range(2):
            owner = 2 * c + jnp.bitwise_xor(odd, slot)
            at = pl.multiple_of(lax.rem(owner - chip + 4, 4) * ROWS, ROWS)
            rows[pl.ds(at, ROWS), :] = source[slot * ROWS : (slot + 1) * ROWS, :]
    width = 4 * ROWS
    for k in range(weights.shape[0] // width):
        product = nt(rows[...], weights[k * width : (k + 1) * width]).astype(BF)
        for i in range(4):
            outs[i][:, k * width : (k + 1) * width] = product[i * ROWS : (i + 1) * ROWS]


def project_query(info, own, arrived, dq, other, weights):
    vmem = pl.BlockSpec(memory_space=pltpu.VMEM)
    width, dims = weights.shape
    return pl.pallas_call(
        project_query_kernel,
        out_shape=(jax.ShapeDtypeStruct((ROWS, width), BF),) * 4
        + (
            jax.ShapeDtypeStruct((BACK,) + own.shape[1:], F32),
            jax.ShapeDtypeStruct(own.shape[1:], BF),
        ),
        in_specs=[pl.BlockSpec(memory_space=pltpu.SMEM)]
        + [vmem] * 5,
        out_specs=(vmem,) * 6,
        scratch_shapes=[pltpu.VMEM((4 * ROWS, dims), BF)],
        compiler_params=pltpu.CompilerParams(vmem_limit_bytes=24 * 1024 * 1024),
        cost_estimate=pl.CostEstimate(
            flops=8 * ROWS * width * dims, bytes_accessed=4 << 20, transcendentals=0
        ),
        name="project_query",
    )(info, own, arrived, dq, other, weights)


def project_kernel(grad, weights, *refs):
    *terms, out = refs
    total = nt(grad[...], weights[...])
    for term in terms:
        total = total + term[...].astype(F32)
    out[0] = total.astype(BF)


def project(grad, weights, terms, n):
    width, dims = weights.shape
    width = width // n
    return pl.pallas_call(
        project_kernel,
        grid=(n,),
        out_shape=jax.ShapeDtypeStruct((n, ROWS, width), BF),
        in_specs=[pl.BlockSpec((ROWS, dims), lambda k: (0, 0))]
        + [pl.BlockSpec((width, dims), lambda k: (k, 0))]
        + [pl.BlockSpec((ROWS, width), lambda k: (0, k))] * len(terms),
        out_specs=pl.BlockSpec((1, ROWS, width), lambda k: (k, 0, 0)),
        compiler_params=pltpu.CompilerParams(vmem_limit_bytes=58 * 1024 * 1024),
        cost_estimate=pl.CostEstimate(
            flops=2 * n * ROWS * width * dims, bytes_accessed=8 << 20, transcendentals=0
        ),
        name="project_kv",
    )(grad, weights, *terms)


def assemble_kernel(where, mine, theirs, out):
    n, _, width = mine.shape
    for k in range(n):
        near = pl.multiple_of((2 * k + where[0]) * width, width)
        far = pl.multiple_of((2 * k + 1 - where[0]) * width, width)
        out[:, pl.ds(near, width)] = mine[k]
        out[:, pl.ds(far, width)] = theirs[k]


def assemble(where, mine, theirs):
    vmem = pl.BlockSpec(memory_space=pltpu.VMEM)
    n, rows, width = mine.shape
    return pl.pallas_call(
        assemble_kernel,
        out_shape=jax.ShapeDtypeStruct((rows, 2 * n * width), BF),
        in_specs=[pl.BlockSpec(memory_space=pltpu.SMEM), vmem, vmem],
        out_specs=vmem,
        compiler_params=pltpu.CompilerParams(vmem_limit_bytes=16 * 1024 * 1024),
        name="assemble",
    )(where, mine, theirs)


def body(queries, key_rows, saved_value_rows, out_grad, doc_lens, w_query, key_weight, value_weight):
    servers = lax.axis_size("server")
    dps = lax.axis_size("dp")
    server = lax.axis_index("server")
    core = lax.axis_index("section")
    odd = server % 2
    both = ("server", "section")

    def swap_pairs(j):
        pairs = []
        for s in range(servers):
            z, a, b = s // 4, (s % 4) // 2, s % 2
            for c in range(2):
                target = z * 4 + 2 * c + (b ^ j)
                pairs.append((2 * s + c, 2 * target + a))
        return pairs

    pairs = [swap_pairs(0), swap_pairs(1)]

    def swap(x, j):
        return lax.ppermute(x, both, pairs[j])

    def shift(x, axis, k):
        n = lax.axis_size(axis)
        return lax.ppermute(x, axis, [(i, (i + k) % n) for i in range(n)])

    def flip(x):
        return lax.ppermute(x, "section", [(0, 1), (1, 0)])

    def groups(left, right):
        half = left.shape[-1] // 2
        first = jnp.concatenate([left[:, :half], right[:, :half]], 1)
        second = jnp.concatenate([left[:, half:], right[:, half:]], 1)
        return jnp.where(odd == 0, first, second), jnp.where(odd == 0, second, first)

    kv_first, kv_second = groups(key_rows[0], saved_value_rows[0])
    block = jnp.concatenate([swap(kv_first, 0), swap(kv_second, 1)], 0)
    blocks = [block]

    queries, out_grad, _ = lax.optimization_barrier((queries, out_grad, block))
    qg_first, qg_second = groups(queries[0], out_grad[0])
    qg0, qg1 = swap(qg_first, 0), swap(qg_second, 1)

    kw_first, kw_second = groups(key_weight, value_weight)
    half = w_query.shape[1] // 2
    weight = jnp.concatenate(
        [kw_first, kw_second, jnp.where(odd == 0, w_query[:, :half], w_query[:, half:])], 1
    )
    half = weight.shape[0] // 2
    mine = jnp.where(core == 0, weight[:half], weight[half:])
    theirs = flip(jnp.where(core == 0, weight[half:], weight[:half]))
    half = 2 * kw_first.shape[1]
    after, _ = lax.optimization_barrier((core, block))
    query_weight = jnp.where(after == (server % 4) // 2, mine[:, half:], theirs[:, half:])
    query_weight = lax.all_gather(query_weight, "dp", axis=0, tiled=True)
    kv_weight = jnp.concatenate(
        [mine[:, :half], jnp.where(after >= 0, theirs[:, :half], mine[:, :half])], 1
    )
    kv_weight = lax.all_gather(kv_weight, "dp", axis=0, tiled=True)

    for k in range(1, BACK + 1):
        if k == BACK:
            blocks[-1], qg0, qg1 = lax.optimization_barrier((blocks[-1], qg0, qg1))
        blocks.append(shift(blocks[-1], "server", 4))
    low = jnp.stack(blocks[:BACK])
    high = jnp.stack(blocks[1:])
    other = flip(jnp.where(core == 0, low, high))

    info = jnp.concatenate(
        [
            jnp.stack([(server // 4) * (4 * ROWS), core, odd, server % 4]).astype(jnp.int32),
            jnp.zeros((4,), jnp.int32),
            doc_lens[0].astype(jnp.int32),
        ]
    )
    dq, own_part, other_part = attention(
        info, qg0, qg1, blocks, other, []
    )

    *sent_products, totals, held = project_query(
        info, own_part, flip(other_part), dq, flip(dq), query_weight
    )
    products = [sent_products[0]]
    for k in range(1, 4):
        pairs_x = [(s, s // 4 * 4 + (s + k) % 4) for s in range(servers)]
        products.append(lax.ppermute(sent_products[k], "server", pairs_x))

    for k in range(BACK - 1, -1, -1):
        if k == 1:
            held, products[1], products[3] = lax.optimization_barrier(
                (held, products[1], products[3])
            )
        held = (totals[k] + shift(held, "server", -4).astype(F32)).astype(BF)
    held, products[2] = lax.optimization_barrier((held, products[2]))
    kv_grad = jnp.concatenate([swap(held[:ROWS], 0), swap(held[ROWS:], 1)], 1)
    kv_grad = jnp.concatenate([kv_grad, flip(kv_grad)], 1)
    mine = project(kv_grad, kv_weight, products, dps)
    theirs = flip(mine)
    where = core.astype(jnp.int32)[None]
    return assemble(where, mine, theirs)[None]


def solution(mesh):
    return jax.shard_map(
        body,
        mesh=mesh,
        in_specs=(
            P("dp", "server", "section"),
            P("dp", "server", "section"),
            P("dp", "server", "section"),
            P("dp", "server", "section"),
            P("dp", None),
            P("dp", "section"),
            P("dp", "section"),
            P("dp", "section"),
        ),
        out_specs=P("dp", "server", None),
        check_vma=False,
    )
```
